128 devices in a mesh: seq: 16 (over x, y_lo, core), tp: 8 (over z, y_hi).
Axes of the slice: x: 4, y: 4 (y_hi: 2, y_lo: 2; y = y_hi * 2 + y_lo), z: 4, core: 2. Of those that a mesh axis runs over, the one named last changes fastest.
Arguments:
- item_states: bfloat16 [32768, 2048], P(('seq', 'tp')), may hold values from -6 to 6
- item_gain: float32 [2048], replicated, may hold values from 0.1 to 1.9
- adapter: bfloat16 [2048, 4096], P(('seq', 'tp')), may hold values from -0.125 to 0.125
- send_rows: int32 [16, 128, 4], P(None, ('seq', 'tp')), may hold values from 0 to 255, as said below
- hist_slot: int32 [16384], P('seq'), may hold values from 0 to 511
- hist_lengths: int32 [4], replicated, may hold values from 1 to 12288, 16384 in all
- user_gain: float32 [4096], replicated, may hold values from 0.1 to 1.9
- w_query: bfloat16 [4096, 2048], P(None, 'tp')
- w_key: bfloat16 [4096, 2048], P(None, 'tp')
- w_value: bfloat16 [4096, 2048], P(None, 'tp'), may hold values from -0.09375 to 0.09375
Outputs:
- attended: bfloat16 [16384, 2048], P('seq', 'tp')
The draws below stay inside these ranges and needn't reach their ends.
Inputs may be any that keep to these rules, and one draw needn't show every extreme that they name: Within each block send_rows[s, r, :] the 4 entries are distinct rows of device r's 256 items. `hist_slot`: slot r * 4 + c names the c-th row that device r sends to the position's seq index. `hist_lengths`: they sum to 16384.
All inputs are finite; a program needn't handle non-finite values.
Results may differ from the reference program's by a relative error of at most 0.012.
Values may be sent and summed in bfloat16 or wider, within the bound.
A program may use at most 128 MiB of HBM per device.

```python
import math
import jax
import jax.numpy as jnp
import numpy as np
from jax import lax

D_ITEM = 2048
D = 4096
HEADS = 16
HD = 128
USERS = 4
ITEM_DEV = 256
TOK_SEQ = 1024
CAP = 4
TOKENS = 16384
ITEMS = 32768
SLOTS = 512
LONGEST = 12288
DEVICES = 128


def shared_query(key):
    inner = jax.random.fold_in(key, 11)
    return jnp.clip(jax.random.normal(inner, (D, HEADS * HD), jnp.float32), -4.0, 4.0)


def draw_w_query(key, part):
    base = shared_query(key)
    return (base * D ** (-0.5)).astype(jnp.bfloat16)


def draw_w_key(key, part):
    key = jax.random.fold_in(key, 23)
    own = jnp.clip(jax.random.normal(key, (D, HEADS * HD), jnp.float32), -4.0, 4.0)
    mixed = own
    return (mixed * D ** (-0.5)).astype(jnp.bfloat16)


def draw_send_rows(key, part):
    key = jax.random.fold_in(key, 7)
    nseq = TOKENS // TOK_SEQ
    keys = jax.random.split(key, nseq * DEVICES)
    rows = jax.vmap(lambda single: jax.random.permutation(single, ITEM_DEV)[:CAP])(keys)
    return rows.reshape(nseq, DEVICES, CAP).astype(jnp.int32)


def set_ends(values, rng, low, high):
    longest = values.shape.index(max(values.shape))
    spots = []
    for shift in (0, 1):
        where = [jax.random.randint(jax.random.fold_in(rng, axis), (), 0, length) for axis, length in enumerate(values.shape)]
        where[longest] = (where[longest] + shift) % values.shape[longest]
        spots.append(tuple(where))
    return values.at[spots[0]].set(low).at[spots[1]].set(high)


def block_levels(rng, extent, shards, low, top_value):
    level = 1.0
    for position, blocks in shards:
        draws = jax.random.uniform(jax.random.fold_in(jax.random.fold_in(rng, 6), position), (blocks,), jnp.float32, low / len(shards), top_value / len(shards))
        level = level * jnp.repeat(jnp.exp(draws), extent[position] // blocks).reshape((-1,) + (1,) * (len(extent) - 1 - position))
    return level


def rank_bounds(amount, skew):
    loads = [(1 << 20) // math.isqrt(grade ** skew) + 1 for grade in range(1, amount + 1)]
    spread = 1 + sum(loads) // (1 << 30)
    return np.cumsum(np.array([max(1, weight // spread) for weight in loads]))


def skewed_ids(key, extent, count, slope):
    table = rank_bounds(count, slope)
    lot = jax.random.randint(jax.random.fold_in(key, 1), extent, 0, int(table[count - 1]))
    rank = jnp.searchsorted(jnp.asarray(table, jnp.int32), lot, side="right")
    return jax.random.permutation(jax.random.fold_in(key, 2), count)[rank].astype(jnp.int32)


def split_up(number_of, total, bound, skew):
    portions = [(1 << 20) // math.isqrt(standing ** skew) + 1 for standing in range(2, number_of + 1)]
    spare, holding = total - bound - (number_of - 1), [1] * (number_of - 1)
    while spare > 0:
        candidates = [i for i in range(number_of - 1) if holding[i] < bound]
        pool, left = sum([portions[i] for i in candidates]), spare
        for i in candidates:
            extra = min(bound - holding[i], max(1, left * portions[i] // pool), spare)
            holding[i] = holding[i] + extra
            spare = spare - extra
    return np.array([bound] + holding)


def uneven_parts(rng, count, total, limit, slope):
    if count == 2:
        one = jax.random.randint(rng, (), max(1, total - limit), min(limit, total - 1) + 1)
        return jnp.stack([one, total - one])
    lengths = jnp.asarray(split_up(count, total, limit, slope), jnp.int32)
    twos = (count - 1) // 2
    donor, sink = lengths[1:1 + 2 * twos:2], lengths[2:2 + 2 * twos:2]
    slack = jnp.minimum(donor - 1, limit - sink)
    moved = jax.random.randint(jax.random.fold_in(rng, 1), (twos,), 0, 1 << 20) % (slack + 1)
    lengths = lengths.at[1:1 + 2 * twos:2].set(donor - moved).at[2:2 + 2 * twos:2].set(sink + moved)
    return lengths[jax.random.permutation(jax.random.fold_in(rng, 2), count)]


def scatter_about(key, extent, deviation, bound, cuts=(), kind=jnp.bfloat16):
    loudness = block_levels(key, extent, cuts, -0.22, 0.18) if cuts else 1.0
    entries = jax.random.normal(key, extent, jnp.float32) * deviation * loudness
    return jnp.minimum(jnp.maximum(entries, -bound), bound).astype(kind)


def setup_inputs(seed: int = 0) -> dict:
    streams_of = jax.random.split(jax.random.key(seed), 11)
    item_states = scatter_about(streams_of[0], (ITEMS, D_ITEM), 1.0, 6.0, ((0, 128),))
    item_gain = jnp.clip(1.0 + 0.18 * jax.random.normal(streams_of[1], (D_ITEM,), jnp.float32), 0.1, 1.9)
    adapter = scatter_about(streams_of[2], (D_ITEM, D), D_ITEM ** -0.5, 0.125, ((0, 128),))
    send_rows = draw_send_rows(jax.random.fold_in(streams_of[10], 71), 0)
    hist_slot = set_ends(skewed_ids(streams_of[4], (TOKENS,), SLOTS, 1), jax.random.fold_in(streams_of[4], 3), 0, SLOTS - 1).astype(jnp.int32)
    hist_lengths = uneven_parts(streams_of[5], USERS, TOKENS, LONGEST, 2).astype(jnp.int32)
    user_gain = jnp.clip(1.0 + 0.18 * jax.random.normal(streams_of[6], (D,), jnp.float32), 0.1, 1.9)
    w_query = draw_w_query(jax.random.fold_in(streams_of[10], 71), 0)
    w_key = draw_w_key(jax.random.fold_in(streams_of[10], 71), 0)
    w_value = scatter_about(streams_of[9], (D, HEADS * HD), D ** -0.5, 0.09375, ((1, 8),))
    return dict(item_states=item_states, item_gain=item_gain, adapter=adapter, send_rows=send_rows, hist_slot=hist_slot, hist_lengths=hist_lengths, user_gain=user_gain, w_query=w_query, w_key=w_key, w_value=w_value)


def normed(values, gain):
    wide = values.astype(jnp.float32)
    factor = lax.rsqrt(lax.optimization_barrier(jnp.mean(wide * wide, axis=-1, keepdims=True)) + 1e-05)
    return (wide * factor * gain.astype(jnp.float32)).astype(jnp.bfloat16)

def reference(item_states, item_gain, adapter, send_rows, hist_slot, hist_lengths, user_gain, w_query, w_key, w_value):
    nseq = TOKENS // TOK_SEQ
    item_norm = normed(item_states, item_gain)
    offsets = (jnp.arange(DEVICES, dtype=jnp.int32) * ITEM_DEV)[None, :, None]
    rows = (offsets + send_rows).reshape(-1).astype(jnp.int32)
    picked = jnp.take(item_norm, rows, axis=0)
    received = jnp.dot(picked, adapter, preferred_element_type=jnp.float32).astype(jnp.bfloat16)
    received = received.reshape(nseq, SLOTS, D)
    shard_of = jnp.arange(TOKENS, dtype=jnp.int32) // TOK_SEQ
    history = received[shard_of, hist_slot]
    hist_norm = normed(history, user_gain)
    query = jnp.dot(hist_norm, w_query, preferred_element_type=jnp.float32).astype(jnp.bfloat16)
    key = jnp.dot(hist_norm, w_key, preferred_element_type=jnp.float32).astype(jnp.bfloat16)
    value = jnp.dot(hist_norm, w_value, preferred_element_type=jnp.float32).astype(jnp.bfloat16)
    ends = jnp.cumsum(hist_lengths).astype(jnp.int32)
    positions = jnp.arange(TOKENS, dtype=jnp.int32)
    user = lax.optimization_barrier(jnp.sum((positions[:, None] >= ends[None, :]).astype(jnp.int32), axis=1)).astype(jnp.int32)
    qwide = query.astype(jnp.float32)
    kwide = key.astype(jnp.float32)
    vwide = value.astype(jnp.float32)
    block = math.gcd(TOKENS, 512)
    nblocks = TOKENS // block
    scale = 1.0 / math.sqrt(HD)

    def attend_block(index):
        bnum = (index // HEADS).astype(jnp.int32)
        head = (index % HEADS).astype(jnp.int32)
        first = (bnum * block).astype(jnp.int32)
        col = (head * HD).astype(jnp.int32)
        qblock = lax.dynamic_slice(qwide, (first, col), (block, HD))
        khead = lax.dynamic_slice(kwide, (jnp.int32(0), col), (TOKENS, HD))
        vhead = lax.dynamic_slice(vwide, (jnp.int32(0), col), (TOKENS, HD))
        scores = jnp.dot(qblock, khead.T, precision=lax.Precision.HIGHEST) * scale
        qpos = first + jnp.arange(block, dtype=jnp.int32)
        quser = lax.dynamic_slice(user, (first,), (block,))
        allowed = (positions[None, :] <= qpos[:, None]) & (user[None, :] == quser[:, None])
        scores = jnp.where(allowed, scores, jnp.float32(-1e+30))
        largest = lax.optimization_barrier(jnp.max(scores, axis=1, keepdims=True))
        prob = jnp.where(allowed, jnp.exp(scores - largest), jnp.float32(0.0))
        total = lax.optimization_barrier(jnp.sum(prob, axis=1, keepdims=True))
        weight = lax.optimization_barrier(prob.astype(jnp.bfloat16)).astype(jnp.float32)
        return jnp.dot(weight, vhead, precision=lax.Precision.HIGHEST) / total
    outputs = lax.map(attend_block, jnp.arange(nblocks * HEADS, dtype=jnp.int32))
    outputs = outputs.reshape(nblocks, HEADS, block, HD).transpose(0, 2, 1, 3)
    return outputs.reshape(TOKENS, HEADS * HD).astype(jnp.bfloat16)
```

```python
import math

import jax
import jax.numpy as jnp
from jax import lax
from jax.experimental import pallas as pl
from jax.experimental.pallas import tpu as pltpu
from jax.sharding import PartitionSpec as P

MESH = pl.DeviceIdType.MESH
HD = 128
USERS = 4
EPS = 1e-05
LOG2E = 1.4426950408889634
EMPTY = -1e30
FLOOR = -1e25
BF = jnp.bfloat16
F32 = jnp.float32


def dot(a, b):
    return jnp.dot(a, b, preferred_element_type=F32)


class Group:
    def __init__(self, axis):
        s, t = lax.axis_index("seq"), lax.axis_index("tp")
        if axis == "seq":
            ring, pair, core = s // 4, (s // 2) % 2, s % 2
            self.block = lambda dr=0, dp=0, ds=0: (
                ((ring + dr) % 4) * 4 + ((pair + dp) % 2) * 2 + (core + ds) % 2
            )
            self.device = lambda *d: (self.block(*d), t)
            self.cores = True
        else:
            ring, pair = t // 2, t % 2
            self.block = lambda dr=0, dp=0: ((ring + dr) % 4) * 2 + (pair + dp) % 2
            self.device = lambda *d: (s, self.block(*d))
            self.cores = False
        self.right, self.left, self.pair = self.device(1, 0), self.device(3, 0), self.device(0, 1)
        self.sib = self.device(0, 0, 1) if self.cores else None


class Gather:
    def __init__(self, group, buf, half, send, recv):
        self.g, self.buf, self.half, self.send, self.recv = group, buf, half, send, recv
        self.count, self.sent = 0, []

    def view(self, index, part=None):
        ref = self.buf.at[index]
        if part is None:
            return ref
        axis, cut, end = self.half
        piece = pl.ds(0, cut) if part == 0 else pl.ds(cut, end - cut)
        return ref.at[(slice(None),) * axis + (piece,)]

    def push(self, index, device, slot, part=None):
        ref = self.view(index, part)
        copy = pltpu.make_async_remote_copy(
            src_ref=ref,
            dst_ref=ref,
            send_sem=self.send.at[self.count],
            recv_sem=self.recv.at[slot],
            device_id=device,
            device_id_type=MESH,
        )
        copy.start()
        self.count += 1
        self.sent.append(copy)

    def got(self, index, slot, part=None):
        ref = self.view(index, part)
        pltpu.make_async_remote_copy(
            src_ref=ref,
            dst_ref=ref,
            send_sem=self.send.at[0],
            recv_sem=self.recv.at[slot],
            device_id=self.g.right,
            device_id_type=MESH,
        ).wait_recv()

    def finish(self):
        for copy in self.sent:
            copy.wait_send()


class PairFirst(Gather):
    def start(self):
        g = self.g
        own = g.block()
        self.push(own, g.pair, 0)
        self.push(own, g.right, 1)
        self.push(own, g.left, 3)
        if g.cores:
            self.push(own, g.sib, 9)

    def from_pair(self):
        g = self.g
        block = g.block(0, 1)
        self.got(block, 0)
        self.push(block, g.right, 2)
        self.push(block, g.left, 4)
        if g.cores:
            self.push(block, g.sib, 10)

    def from_ring(self):
        g = self.g
        for dp in (0, 1):
            block = g.block(3, dp)
            self.got(block, 1 + dp)
            self.push(block, g.right, 5 + dp, 0)
            if g.cores:
                self.push(block, g.sib, 11 + dp)
            block = g.block(1, dp)
            self.got(block, 3 + dp)
            self.push(block, g.left, 7 + dp, 1)
            if g.cores:
                self.push(block, g.sib, 13 + dp)

    def from_far(self):
        g = self.g
        for dp in (0, 1):
            block = g.block(2, dp)
            self.got(block, 5 + dp, 0)
            self.got(block, 7 + dp, 1)
            if g.cores:
                self.push(block, g.sib, 15 + dp)

    def sib_own(self):
        for dp in (0, 1):
            self.got(self.g.block(0, dp, 1), 9 + dp)

    def sib_ring(self):
        for dp in (0, 1):
            self.got(self.g.block(3, dp, 1), 11 + dp)
            self.got(self.g.block(1, dp, 1), 13 + dp)

    def sib_far(self):
        for dp in (0, 1):
            self.got(self.g.block(2, dp, 1), 15 + dp)


class RingFirst(Gather):
    def start(self):
        g = self.g
        own = g.block()
        self.push(own, g.right, 1)
        self.push(own, g.left, 2)
        self.push(own, g.pair, 0)
        self.push(own, g.sib, 8)

    def from_pair(self):
        block = self.g.block(0, 1)
        self.got(block, 0)
        self.push(block, self.g.sib, 9)

    def from_ring(self):
        g = self.g
        block = g.block(3, 0)
        self.got(block, 1)
        self.push(block, g.right, 3, 0)
        self.push(block, g.pair, 5)
        self.push(block, g.sib, 10)
        block = g.block(1, 0)
        self.got(block, 2)
        self.push(block, g.left, 4, 1)
        self.push(block, g.pair, 6)
        self.push(block, g.sib, 11)

    def from_far(self):
        g = self.g
        block = g.block(2, 0)
        self.got(block, 3, 0)
        self.got(block, 4, 1)
        self.push(block, g.pair, 7)
        self.push(block, g.sib, 12)

    def pair_ring(self):
        g = self.g
        block = g.block(3, 1)
        self.got(block, 5)
        self.push(block, g.sib, 13)
        block = g.block(1, 1)
        self.got(block, 6)
        self.push(block, g.sib, 14)

    def pair_far(self):
        g = self.g
        block = g.block(2, 1)
        self.got(block, 7)
        self.push(block, g.sib, 15)

    def sib_own(self):
        g = self.g
        self.got(g.block(0, 0, 1), 8)
        self.got(g.block(0, 1, 1), 9)

    def sib_ring(self):
        g = self.g
        self.got(g.block(3, 0, 1), 10)
        self.got(g.block(1, 0, 1), 11)
        self.got(g.block(3, 1, 1), 13)
        self.got(g.block(1, 1, 1), 14)

    def sib_far(self):
        g = self.g
        self.got(g.block(2, 0, 1), 12)
        self.got(g.block(2, 1, 1), 15)


def pieces(values):
    first = values.astype(BF).astype(F32)
    second = (values - first).astype(BF).astype(F32)
    return first, second, values - first - second


def kernel(
    lengths,
    items,
    item_gain,
    adapter,
    picks,
    slot_row,
    slot_col,
    user_gain,
    w_query,
    w_key,
    w_value,
    out,
    abuf,
    scaled,
    weights,
    spread,
    xs,
    xa,
    xb,
    rows,
    mix,
    ebuf,
    raw,
    sums,
    query,
    kt,
    val,
    place,
    place_t,
    qpos,
    kpos_t,
    vpos,
    near,
    near_log,
    top,
    accum,
    w_sem,
    a_send,
    a_recv,
    r_send,
    r_recv,
    x_send,
    x_recv,
    m_send,
    m_recv,
    e_send,
    e_recv,
    s_send,
    s_recv,
    k_send,
    k_recv,
    v_send,
    v_recv,
):
    seq, tp = lax.axis_index("seq"), lax.axis_index("tp")
    nseq, ntp = lax.axis_size("seq"), lax.axis_size("tp")
    wide = adapter.shape[1]
    nslot, ditem = rows.shape
    chunks = ditem // HD
    ecols = ebuf.shape[2]
    hcols = w_query.shape[1]
    heads = hcols // HD
    npos = out.shape[0]
    nchosen = xs.shape[0]
    cap = nchosen // nseq
    first_pos = seq * npos

    loads = []
    for i, ref in enumerate((w_query, w_key, w_value)):
        load = pltpu.make_async_copy(ref, weights.at[i], w_sem.at[i])
        load.start()
        loads.append(load)

    barrier = pltpu.get_barrier_semaphore()
    for k in range(1, ntp):
        peer = (seq, lax.rem(tp + k, ntp))
        pl.semaphore_signal(barrier, inc=1, device_id=peer, device_id_type=MESH)
    for k in range(1, nseq):
        peer = (lax.rem(seq + k, nseq), tp)
        pl.semaphore_signal(barrier, inc=1, device_id=peer, device_id_type=MESH)

    pick = (lax.broadcasted_iota(jnp.int32, (nchosen, items.shape[0]), 1) == picks[...]).astype(BF)
    chosen = dot(pick, items[...])
    factor = lax.rsqrt(jnp.mean(chosen * chosen, axis=1, keepdims=True) + EPS)
    chosen = chosen * factor * item_gain[...]
    for k in range(chunks):
        spread[pl.ds(k, nchosen, stride=chunks), :] = chosen[:, k * HD : (k + 1) * HD]
    xs[...] = spread[: nchosen * chunks].reshape(nchosen, chunks, HD).astype(BF)

    pl.semaphore_wait(barrier, ntp + nseq - 2)

    over_tp, over_seq = Group("tp"), Group("seq")

    abuf[tp] = adapter[...]
    ga = PairFirst(over_tp, abuf, (1, wide // 2, wide), a_send, a_recv)
    ga.start()
    routed = []
    for k in range(1, nseq):
        peer = lax.rem(seq + k, nseq)
        copy = pltpu.make_async_remote_copy(
            src_ref=xs.at[pl.ds(peer * cap, cap)],
            dst_ref=xa.at[seq],
            send_sem=r_send.at[k],
            recv_sem=r_recv.at[k],
            device_id=(peer, tp),
            device_id_type=MESH,
        )
        copy.start()
        routed.append(copy)
    xa[seq] = xs[pl.ds(seq * cap, cap)]

    ends = [lengths[0]]
    for u in range(1, USERS):
        ends.append(ends[-1] + lengths[u])
    row_pos = lax.broadcasted_iota(jnp.int32, (1, npos), 1) + first_pos
    col_pos = lax.broadcasted_iota(jnp.int32, (npos, 1), 0) + first_pos

    def user_of(pos):
        total = jnp.zeros_like(pos)
        for end in ends:
            total = total + jnp.where(pos >= end, 1, 0)
        return total

    begin = jnp.zeros_like(col_pos)
    for end in ends:
        begin = jnp.maximum(begin, jnp.where(col_pos >= end, end, 0))
    place[...] = (lax.broadcasted_iota(jnp.int32, (npos, nslot), 1) == slot_col[...]).astype(BF)
    place_t[...] = (lax.broadcasted_iota(jnp.int32, (nslot, npos), 0) == slot_row[...]).astype(BF)
    belongs = lax.broadcasted_iota(jnp.int32, (16, npos), 0) % USERS == user_of(row_pos)
    held = dot(belongs.astype(BF), place[...])
    weigh = jnp.where(held > 0.5, jnp.log(jnp.maximum(held, 1.0)) * LOG2E, EMPTY)
    parts = pieces(weigh)
    part = lax.broadcasted_iota(jnp.int32, (16, nslot), 0) // USERS
    weigh = jnp.where(part == 0, parts[0], jnp.where(part == 1, parts[1], jnp.where(part == 2, parts[2], 0.0)))
    kt[seq, hcols:, :] = weigh.astype(BF)

    ga.from_pair()
    for k in range(1, nseq):
        pltpu.make_async_remote_copy(
            src_ref=xa.at[0],
            dst_ref=xa.at[lax.rem(seq + nseq - k, nseq)],
            send_sem=r_send.at[k],
            recv_sem=r_recv.at[k],
            device_id=(lax.rem(seq + k, nseq), tp),
            device_id_type=MESH,
        ).wait_recv()
    xb[tp] = xa[...]
    gx = PairFirst(over_tp, xb, (0, nseq // 2, nseq), x_send, x_recv)
    gx.start()
    ga.from_ring()
    ga.from_far()

    arows = ntp * adapter.shape[0]
    for k in range(ntp):
        ebuf[seq, k * adapter.shape[0] : (k + 1) * adapter.shape[0], :] = abuf[
            k, :, pl.ds(pl.multiple_of(tp * ecols, HD), ecols)
        ]
    ge = RingFirst(over_seq, ebuf, (0, arows // 2, arows), e_send, e_recv)
    ge.start()
    scaled[...] = (abuf[...].reshape(arows, wide).astype(F32) * user_gain[...]).astype(BF)
    for i, load in enumerate(loads):
        load.wait()
        mix[seq, :, i * hcols : (i + 1) * hcols] = dot(scaled[...], weights[i]).astype(BF)
    gm = PairFirst(over_seq, mix, (0, arows // 2, arows), m_send, m_recv)
    gm.start()

    gx.from_pair()
    ge.from_pair()
    gm.from_pair()
    ge.from_ring()
    gx.from_ring()
    gm.from_ring()
    ge.pair_ring()
    gx.from_far()
    for k in range(ntp):
        size = nchosen * chunks
        spread[pl.ds(k * size, size), :] = xb[k].reshape(size, HD).astype(F32)
    for k in range(chunks):
        rows[:, k * HD : (k + 1) * HD] = spread[pl.ds(k, nslot, stride=chunks), :].astype(BF)
    ge.from_far()
    gm.from_far()
    ge.pair_far()
    for gather in (ge, gm):
        gather.sib_own()
        gather.sib_ring()
        gather.sib_far()

    square = jnp.zeros((nslot, HD), F32)
    tile = min(256, ecols)
    for j in range(ecols // tile):
        emb = dot(rows[...], ebuf[:, :, j * tile : (j + 1) * tile].reshape(ditem, tile))
        for i in range(tile // HD):
            piece = emb[:, i * HD : (i + 1) * HD]
            square = square + piece * piece
    sums[tp] = jnp.broadcast_to(jnp.sum(square.T, axis=0, keepdims=True), (8, nslot))
    shared = []
    for k in range(1, ntp):
        copy = pltpu.make_async_remote_copy(
            src_ref=sums.at[tp],
            dst_ref=sums.at[tp],
            send_sem=s_send.at[k],
            recv_sem=s_recv.at[k],
            device_id=(seq, lax.rem(tp + k, ntp)),
            device_id_type=MESH,
        )
        copy.start()
        shared.append(copy)
    for i in range(3):
        raw[i] = dot(rows[...], mix[:, :, i * hcols : (i + 1) * hcols].reshape(ditem, hcols))
    for k in range(1, ntp):
        other = lax.rem(tp + ntp - k, ntp)
        pltpu.make_async_remote_copy(
            src_ref=sums.at[other],
            dst_ref=sums.at[other],
            send_sem=s_send.at[k],
            recv_sem=s_recv.at[k],
            device_id=(seq, lax.rem(tp + k, ntp)),
            device_id_type=MESH,
        ).wait_recv()
    total = sums[0]
    for k in range(1, ntp):
        total = total + sums[k]
    inverse = lax.rsqrt(total[0:1, :] / wide + EPS)
    down = jnp.broadcast_to(inverse, (HD, nslot)).T
    for h in range(heads):
        span = slice(h * HD, (h + 1) * HD)
        kt[seq, span, :] = (raw[1, :, span].T * inverse).astype(BF)
        val[seq, :, span] = (raw[2, :, span] * down).astype(BF)
        query[:, span] = (raw[0, :, span] * (down * (LOG2E / math.sqrt(HD)))).astype(BF)
    gk = PairFirst(over_seq, kt, (0, hcols // 2, kt.shape[1]), k_send, k_recv)
    gv = RingFirst(over_seq, val, (0, nslot // 2, nslot), v_send, v_recv)
    gk.start()
    gv.start()

    qpos[...] = dot(place[...], query[...]).astype(BF)
    vpos[...] = dot(place[...], val[seq]).astype(BF)
    kpos_t[...] = dot(kt[seq, :hcols, :], place_t[...]).astype(BF)
    step = min(256, npos)
    for h in range(heads):
        span = slice(h * HD, (h + 1) * HD)
        for i in range(npos // step):
            here, upto = slice(i * step, (i + 1) * step), (i + 1) * step
            score = dot(qpos[here, span], kpos_t[span, :upto])
            cols = lax.broadcasted_iota(jnp.int32, (step, upto), 1) + first_pos
            allowed = (cols <= col_pos[here]) & (cols >= begin[here])
            score = jnp.where(allowed, score, EMPTY)
            largest = jnp.max(score, axis=1, keepdims=True)
            prob = jnp.exp2(score - largest).astype(BF)
            both = dot(prob, jnp.concatenate([vpos[:upto, span], jnp.ones((upto, HD), BF)], axis=1))
            near[h, here, :] = both[:, :HD] / both[:, HD:]
            near_log[h, here, :] = largest + jnp.log(both[:, HD:]) * LOG2E
    top[...] = jnp.full(top.shape, FLOOR, F32)
    accum[...] = jnp.zeros(accum.shape, F32)

    user_here = user_of(jnp.zeros((16, nslot), jnp.int32) + first_pos)
    which = lax.broadcasted_iota(jnp.int32, (16, nslot), 0)
    chosen_rows = (which % USERS == user_here) & (which < 3 * USERS)
    ones = jnp.ones((nslot, HD), BF)

    def attend(ring):
        def block(i, carry):
            other = ring * 4 + i

            @pl.when(other < seq)
            def _():
                tail = kt[other, hcols:, :].astype(F32)
                bias = jnp.sum(jnp.where(chosen_rows, tail, 0.0), axis=0, keepdims=True)
                for h in range(heads):
                    span = slice(h * HD, (h + 1) * HD)
                    score = dot(query[:, span], kt[other, span, :]) + bias
                    before = top[h]
                    after = jnp.maximum(before, jnp.max(score, axis=1, keepdims=True))
                    prob = jnp.exp2(score - after[:, :1]).astype(BF)
                    shrink = jnp.exp2(before - after)
                    both = dot(prob, jnp.concatenate([val[other, :, span], ones], axis=1))
                    accum[h] = accum[h] * jnp.concatenate([shrink, shrink], axis=1) + both
                    top[h] = after

            return carry

        lax.fori_loop(0, 4, block, 0)

    ring = seq // 4
    gk.from_pair()
    gv.from_pair()
    gk.sib_own()
    gv.sib_own()
    attend(ring)
    gv.from_ring()
    gk.from_ring()
    gv.pair_ring()
    gk.sib_ring()
    gv.sib_ring()
    attend((ring + 3) % 4)
    attend((ring + 1) % 4)
    gv.from_far()
    gk.from_far()
    gv.pair_far()
    gk.sib_far()
    gv.sib_far()
    attend((ring + 2) % 4)

    lane = lax.broadcasted_iota(jnp.int32, (nslot, HD), 1)
    reaches = begin < first_pos
    for h in range(heads):
        span = slice(h * HD, (h + 1) * HD)
        weight = accum[h, :, HD:]
        some = weight > 0.0
        far = accum[h, :, :HD] / jnp.where(some, weight, 1.0)
        far_log = jnp.where(some, top[h] + jnp.log(jnp.where(some, weight, 1.0)) * LOG2E, FLOOR)
        parts = pieces(far_log)
        packed = jnp.where(lane == 0, parts[0], jnp.where(lane == 1, parts[1], jnp.where(lane == 2, parts[2], 0.0)))
        moved = dot(place[...], jnp.concatenate([far.astype(BF), packed.astype(BF)], axis=1))
        far_log = jnp.sum(moved[:, HD:], axis=1, keepdims=True)
        far_log = jnp.where(reaches, far_log, FLOOR)
        near_here = near_log[h]
        both = jnp.maximum(near_here, far_log)
        near_weight = jnp.exp2(near_here - both)
        far_weight = jnp.exp2(far_log - both)
        mean = (near[h] * near_weight + moved[:, :HD] * far_weight) / (near_weight + far_weight)
        out[:, span] = mean.astype(BF)

    for gather in (ga, gx, ge, gm, gk, gv):
        gather.finish()
    for copy in routed + shared:
        copy.wait_send()


def per_device(
    item_states,
    item_gain,
    adapter,
    send_rows,
    hist_slot,
    hist_lengths,
    user_gain,
    w_query,
    w_key,
    w_value,
):
    ntp, nseq = lax.axis_size("tp"), lax.axis_size("seq")
    cap = send_rows.shape[2]
    arows, wide = adapter.shape
    ditem = item_states.shape[1]
    hcols = w_query.shape[1]
    heads = hcols // HD
    npos = hist_slot.shape[0]
    nchosen = nseq * cap
    nslot = ntp * nchosen
    chunks = ditem // HD
    ecols = wide // ntp
    device, column = hist_slot // cap, hist_slot % cap
    slots = ((device % ntp) * nseq + device // ntp) * cap + column
    vmem = pl.BlockSpec(memory_space=pltpu.VMEM)
    hbm = pl.BlockSpec(memory_space=pl.ANY)
    dma = pltpu.SemaphoreType.DMA
    scratch = [
        pltpu.VMEM((ntp, arows, wide), BF),
        pltpu.VMEM((ntp * arows, wide), BF),
        pltpu.VMEM((3, wide, hcols), BF),
        pltpu.VMEM((nslot * chunks, HD), F32),
        pltpu.VMEM((nchosen, chunks, HD), BF),
        pltpu.VMEM((nseq, cap, chunks, HD), BF),
        pltpu.VMEM((ntp, nseq, cap, chunks, HD), BF),
        pltpu.VMEM((nslot, ditem), BF),
        pltpu.VMEM((nseq, ntp * arows, 3 * hcols), BF),
        pltpu.VMEM((nseq, ntp * arows, ecols), BF),
        pltpu.VMEM((3, nslot, hcols), F32),
        pltpu.VMEM((ntp, 8, nslot), F32),
        pltpu.VMEM((nslot, hcols), BF),
        pltpu.VMEM((nseq, hcols + 16, nslot), BF),
        pltpu.VMEM((nseq, nslot, hcols), BF),
        pltpu.VMEM((npos, nslot), BF),
        pltpu.VMEM((nslot, npos), BF),
        pltpu.VMEM((npos, hcols), BF),
        pltpu.VMEM((hcols, npos), BF),
        pltpu.VMEM((npos, hcols), BF),
        pltpu.VMEM((heads, npos, HD), F32),
        pltpu.VMEM((heads, npos, HD), F32),
        pltpu.VMEM((heads, nslot, HD), F32),
        pltpu.VMEM((heads, nslot, 2 * HD), F32),
        dma((3,)),
        dma((9,)),
        dma((9,)),
        dma((nseq,)),
        dma((nseq,)),
        dma((9,)),
        dma((9,)),
        dma((17,)),
        dma((17,)),
        dma((16,)),
        dma((16,)),
        dma((ntp,)),
        dma((ntp,)),
        dma((17,)),
        dma((17,)),
        dma((16,)),
        dma((16,)),
    ]
    return pl.pallas_call(
        kernel,
        out_shape=jax.ShapeDtypeStruct((npos, hcols), BF),
        in_specs=[pl.BlockSpec(memory_space=pltpu.SMEM)] + [vmem] * 7 + [hbm] * 3,
        out_specs=vmem,
        scratch_shapes=scratch,
        compiler_params=pltpu.CompilerParams(
            collective_id=0, has_side_effects=True, vmem_limit_bytes=56 * 1024 * 1024
        ),
    )(
        hist_lengths,
        item_states,
        item_gain.reshape(1, -1),
        adapter,
        send_rows[:, 0, :].reshape(-1, 1),
        slots.reshape(1, -1),
        slots.reshape(-1, 1),
        user_gain.reshape(1, -1),
        w_query,
        w_key,
        w_value,
    )


def solution(mesh):
    in_specs = (
        P(("seq", "tp"), None),
        P(),
        P(("seq", "tp"), None),
        P(None, ("seq", "tp"), None),
        P("seq"),
        P(),
        P(),
        P(None, "tp"),
        P(None, "tp"),
        P(None, "tp"),
    )
    return jax.shard_map(
        per_device, mesh=mesh, in_specs=in_specs, out_specs=P("seq", "tp"), check_vma=False
    )
```

```python
import math

import jax
import jax.numpy as jnp
from jax import lax
from jax.experimental import pallas as pl
from jax.experimental.pallas import tpu as pltpu
from jax.sharding import PartitionSpec as P

MESH = pl.DeviceIdType.MESH
HD = 128
USERS = 4
EPS = 1e-05
LOG2E = 1.4426950408889634
EMPTY = -1e30
FLOOR = -1e25
BF = jnp.bfloat16
F32 = jnp.float32


def dot(a, b):
    return jnp.dot(a, b, preferred_element_type=F32)


class Group:
    def __init__(self, axis):
        s, t = lax.axis_index("seq"), lax.axis_index("tp")
        if axis == "seq":
            ring, pair, core = s // 4, (s // 2) % 2, s % 2
            self.block = lambda dr=0, dp=0, ds=0: (
                ((ring + dr) % 4) * 4 + ((pair + dp) % 2) * 2 + (core + ds) % 2
            )
            self.device = lambda *d: (self.block(*d), t)
            self.cores = True
        else:
            ring, pair = t // 2, t % 2
            self.block = lambda dr=0, dp=0: ((ring + dr) % 4) * 2 + (pair + dp) % 2
            self.device = lambda *d: (s, self.block(*d))
            self.cores = False
        self.right, self.left, self.pair = self.device(1, 0), self.device(3, 0), self.device(0, 1)
        self.sib = self.device(0, 0, 1) if self.cores else None


class Gather:
    def __init__(self, group, buf, half, send, recv):
        self.g, self.buf, self.half, self.send, self.recv = group, buf, half, send, recv
        self.count, self.sent = 0, []

    def view(self, index, part=None):
        ref = self.buf.at[index]
        if part is None:
            return ref
        axis, cut, end = self.half
        piece = pl.ds(0, cut) if part == 0 else pl.ds(cut, end - cut)
        return ref.at[(slice(None),) * axis + (piece,)]

    def push(self, index, device, slot, part=None):
        ref = self.view(index, part)
        copy = pltpu.make_async_remote_copy(
            src_ref=ref,
            dst_ref=ref,
            send_sem=self.send.at[self.count],
            recv_sem=self.recv.at[slot],
            device_id=device,
            device_id_type=MESH,
        )
        copy.start()
        self.count += 1
        self.sent.append(copy)

    def got(self, index, slot, part=None):
        ref = self.view(index, part)
        pltpu.make_async_remote_copy(
            src_ref=ref,
            dst_ref=ref,
            send_sem=self.send.at[0],
            recv_sem=self.recv.at[slot],
            device_id=self.g.right,
            device_id_type=MESH,
        ).wait_recv()

    def finish(self):
        for copy in self.sent:
            copy.wait_send()


class PairFirst(Gather):
    def start(self):
        g = self.g
        own = g.block()
        self.push(own, g.pair, 0)
        self.push(own, g.right, 1)
        self.push(own, g.left, 3)
        if g.cores:
            self.push(own, g.sib, 9)

    def from_pair(self):
        g = self.g
        block = g.block(0, 1)
        self.got(block, 0)
        self.push(block, g.right, 2)
        self.push(block, g.left, 4)
        if g.cores:
            self.push(block, g.sib, 10)

    def from_ring(self):
        g = self.g
        for dp in (0, 1):
            block = g.block(3, dp)
            self.got(block, 1 + dp)
            self.push(block, g.right, 5 + dp, 0)
            if g.cores:
                self.push(block, g.sib, 11 + dp)
            block = g.block(1, dp)
            self.got(block, 3 + dp)
            self.push(block, g.left, 7 + dp, 1)
            if g.cores:
                self.push(block, g.sib, 13 + dp)

    def from_far(self):
        g = self.g
        for dp in (0, 1):
            block = g.block(2, dp)
            self.got(block, 5 + dp, 0)
            self.got(block, 7 + dp, 1)
            if g.cores:
                self.push(block, g.sib, 15 + dp)

    def sib_own(self):
        for dp in (0, 1):
            self.got(self.g.block(0, dp, 1), 9 + dp)

    def sib_ring(self):
        for dp in (0, 1):
            self.got(self.g.block(3, dp, 1), 11 + dp)
            self.got(self.g.block(1, dp, 1), 13 + dp)

    def sib_far(self):
        for dp in (0, 1):
            self.got(self.g.block(2, dp, 1), 15 + dp)


class RingFirst(Gather):
    def start(self):
        g = self.g
        own = g.block()
        self.push(own, g.right, 1)
        self.push(own, g.left, 2)
        self.push(own, g.pair, 0)
        self.push(own, g.sib, 8)

    def from_pair(self):
        block = self.g.block(0, 1)
        self.got(block, 0)
        self.push(block, self.g.sib, 9)

    def from_ring(self):
        g = self.g
        block = g.block(3, 0)
        self.got(block, 1)
        self.push(block, g.right, 3, 0)
        self.push(block, g.pair, 5)
        self.push(block, g.sib, 10)
        block = g.block(1, 0)
        self.got(block, 2)
        self.push(block, g.left, 4, 1)
        self.push(block, g.pair, 6)
        self.push(block, g.sib, 11)

    def from_far(self):
        g = self.g
        block = g.block(2, 0)
        self.got(block, 3, 0)
        self.got(block, 4, 1)
        self.push(block, g.pair, 7)
        self.push(block, g.sib, 12)

    def pair_ring(self):
        g = self.g
        block = g.block(3, 1)
        self.got(block, 5)
        self.push(block, g.sib, 13)
        block = g.block(1, 1)
        self.got(block, 6)
        self.push(block, g.sib, 14)

    def pair_far(self):
        g = self.g
        block = g.block(2, 1)
        self.got(block, 7)
        self.push(block, g.sib, 15)

    def sib_own(self):
        g = self.g
        self.got(g.block(0, 0, 1), 8)
        self.got(g.block(0, 1, 1), 9)

    def sib_ring(self):
        g = self.g
        self.got(g.block(3, 0, 1), 10)
        self.got(g.block(1, 0, 1), 11)
        self.got(g.block(3, 1, 1), 13)
        self.got(g.block(1, 1, 1), 14)

    def sib_far(self):
        g = self.g
        self.got(g.block(2, 0, 1), 12)
        self.got(g.block(2, 1, 1), 15)


def pieces(values):
    first = values.astype(BF).astype(F32)
    second = (values - first).astype(BF).astype(F32)
    return first, second, values - first - second


def kernel(
    lengths,
    items,
    item_gain,
    adapter,
    picks,
    slots,
    user_gain,
    w_query,
    w_key,
    w_value,
    out,
    abuf,
    scaled,
    weights,
    spread,
    xs,
    xa,
    xb,
    rows,
    mix,
    ebuf,
    raw,
    sums,
    query,
    kt,
    val,
    place,
    place_t,
    qpos,
    kpos_t,
    vpos,
    near,
    near_log,
    top,
    accum,
    w_sem,
    a_send,
    a_recv,
    r_send,
    r_recv,
    c_send,
    c_recv,
    x_send,
    x_recv,
    m_send,
    m_recv,
    e_send,
    e_recv,
    s_send,
    s_recv,
    k_send,
    k_recv,
    v_send,
    v_recv,
):
    seq, tp = lax.axis_index("seq"), lax.axis_index("tp")
    nseq, ntp = lax.axis_size("seq"), lax.axis_size("tp")
    wide = adapter.shape[1]
    nslot, ditem = rows.shape
    chunks = ditem // HD
    ecols = ebuf.shape[2]
    hcols = w_query.shape[1]
    heads = hcols // HD
    npos = out.shape[0]
    nchosen = xs.shape[0]
    cap = nchosen // nseq
    first_pos = seq * npos

    loads = []
    for i, ref in enumerate((w_query, w_key, w_value)):
        load = pltpu.make_async_copy(ref, weights.at[i], w_sem.at[i])
        load.start()
        loads.append(load)

    barrier = pltpu.get_barrier_semaphore()
    for k in range(1, ntp):
        peer = (seq, lax.rem(tp + k, ntp))
        pl.semaphore_signal(barrier, inc=1, device_id=peer, device_id_type=MESH)
    for k in range(1, nseq):
        peer = (lax.rem(seq + k, nseq), tp)
        pl.semaphore_signal(barrier, inc=1, device_id=peer, device_id_type=MESH)

    which = lax.broadcasted_iota(jnp.int32, (nchosen, 1), 0)
    column = jnp.zeros((nchosen, 1), jnp.int32)
    for r in range(nchosen):
        column = jnp.where(which == r, picks[r % cap, r // cap], column)
    pick = (lax.broadcasted_iota(jnp.int32, (nchosen, items.shape[0]), 1) == column).astype(BF)
    chosen = dot(pick, items[...])
    factor = lax.rsqrt(jnp.mean(chosen * chosen, axis=1, keepdims=True) + EPS)
    chosen = chosen * factor * item_gain[...]
    for k in range(chunks):
        spread[pl.ds(k, nchosen, stride=chunks), :] = chosen[:, k * HD : (k + 1) * HD]
    xs[...] = spread[: nchosen * chunks].reshape(nchosen, chunks, HD).astype(BF)

    pl.semaphore_wait(barrier, ntp + nseq - 2)

    over_tp, over_seq = Group("tp"), Group("seq")
    arows = adapter.shape[0]

    abuf[tp] = adapter[...]
    ga = PairFirst(over_tp, abuf, (1, wide // 2, wide), a_send, a_recv)
    ga.start()

    def columns_of(index):
        return adapter.at[:, pl.ds(pl.multiple_of(index * ecols, HD), ecols)]

    def column_copy(k, peer, source):
        return pltpu.make_async_remote_copy(
            src_ref=columns_of(peer),
            dst_ref=ebuf.at[seq, pl.ds(pl.multiple_of(source * arows, arows), arows)],
            send_sem=c_send.at[k],
            recv_sem=c_recv.at[k],
            device_id=(seq, peer),
            device_id_type=MESH,
        )

    def routed_copy(k, peer, source):
        return pltpu.make_async_remote_copy(
            src_ref=xs.at[pl.ds(peer * cap, cap)],
            dst_ref=xa.at[source],
            send_sem=r_send.at[k],
            recv_sem=r_recv.at[k],
            device_id=(peer, tp),
            device_id_type=MESH,
        )

    straight = []
    for k in range(1, ntp):
        straight.append(column_copy(k, lax.rem(tp + k, ntp), tp))
        straight[-1].start()
    for k in range(1, nseq):
        straight.append(routed_copy(k, lax.rem(seq + k, nseq), seq))
        straight[-1].start()
    xa[seq] = xs[pl.ds(seq * cap, cap)]
    ebuf[seq, pl.ds(pl.multiple_of(tp * arows, arows), arows), :] = adapter[
        :, pl.ds(pl.multiple_of(tp * ecols, HD), ecols)
    ]

    origin = slots[...] // cap
    spot = ((origin % ntp) * nseq + origin // ntp) * cap + slots[...] % cap
    groups = spot.shape[0]
    spot_t = jnp.concatenate([spot.astype(F32), jnp.zeros((HD - groups, HD), F32)], axis=0).T.astype(jnp.int32)
    for k in range(groups):
        here = slice(k * HD, (k + 1) * HD)
        place_t[:, here] = (lax.broadcasted_iota(jnp.int32, (nslot, HD), 0) == spot[k : k + 1, :]).astype(BF)
        place[here, :] = (lax.broadcasted_iota(jnp.int32, (HD, nslot), 1) == spot_t[:, k : k + 1]).astype(BF)

    ga.from_pair()
    for k in range(1, ntp):
        column_copy(k, lax.rem(tp + k, ntp), lax.rem(tp + ntp - k, ntp)).wait_recv()
    ge = RingFirst(over_seq, ebuf, (0, ntp * arows // 2, ntp * arows), e_send, e_recv)
    ge.start()
    ga.from_ring()
    for k in range(1, nseq):
        routed_copy(k, lax.rem(seq + k, nseq), lax.rem(seq + nseq - k, nseq)).wait_recv()
    xb[tp] = xa[...]
    gx = PairFirst(over_tp, xb, (0, nseq // 2, nseq), x_send, x_recv)
    gx.start()

    ends = [lengths[0]]
    for u in range(1, USERS):
        ends.append(ends[-1] + lengths[u])
    row_pos = lax.broadcasted_iota(jnp.int32, (1, npos), 1) + first_pos
    col_pos = lax.broadcasted_iota(jnp.int32, (npos, 1), 0) + first_pos

    def user_of(pos):
        total = jnp.zeros_like(pos)
        for end in ends:
            total = total + jnp.where(pos >= end, 1, 0)
        return total

    begin = jnp.zeros_like(col_pos)
    for end in ends:
        begin = jnp.maximum(begin, jnp.where(col_pos >= end, end, 0))
    belongs = lax.broadcasted_iota(jnp.int32, (16, npos), 0) % USERS == user_of(row_pos)
    held = dot(belongs.astype(BF), place[...])
    weigh = jnp.where(held > 0.5, jnp.log(jnp.maximum(held, 1.0)) * LOG2E, EMPTY)
    parts = pieces(weigh)
    part = lax.broadcasted_iota(jnp.int32, (16, nslot), 0) // USERS
    weigh = jnp.where(part == 0, parts[0], jnp.where(part == 1, parts[1], jnp.where(part == 2, parts[2], 0.0)))
    kt[seq, hcols:, :] = weigh.astype(BF)

    ga.from_far()
    arows = ntp * arows
    scaled[...] = (abuf[...].reshape(arows, wide).astype(F32) * user_gain[...]).astype(BF)
    for i, load in enumerate(loads):
        load.wait()
        mix[seq, :, i * hcols : (i + 1) * hcols] = dot(scaled[...], weights[i]).astype(BF)
    gm = PairFirst(over_seq, mix, (0, arows // 2, arows), m_send, m_recv)
    gm.start()

    ge.from_pair()
    ge.from_ring()
    gx.from_pair()
    ge.pair_ring()
    gm.from_pair()
    ge.from_far()
    gx.from_ring()
    gm.from_ring()
    ge.pair_far()
    gx.from_far()
    for k in range(ntp):
        size = nchosen * chunks
        spread[pl.ds(k * size, size), :] = xb[k].reshape(size, HD).astype(F32)
    for k in range(chunks):
        rows[:, k * HD : (k + 1) * HD] = spread[pl.ds(k, nslot, stride=chunks), :].astype(BF)
    ge.sib_own()
    ge.sib_ring()
    ge.sib_far()

    square = jnp.zeros((nslot, HD), F32)
    tile = min(256, ecols)
    for j in range(ecols // tile):
        emb = dot(rows[...], ebuf[:, :, j * tile : (j + 1) * tile].reshape(ditem, tile))
        for i in range(tile // HD):
            piece = emb[:, i * HD : (i + 1) * HD]
            square = square + piece * piece
    sums[tp] = jnp.broadcast_to(jnp.sum(square.T, axis=0, keepdims=True), (8, nslot))
    shared = []
    for k in range(1, ntp):
        copy = pltpu.make_async_remote_copy(
            src_ref=sums.at[tp],
            dst_ref=sums.at[tp],
            send_sem=s_send.at[k],
            recv_sem=s_recv.at[k],
            device_id=(seq, lax.rem(tp + k, ntp)),
            device_id_type=MESH,
        )
        copy.start()
        shared.append(copy)
    gm.from_far()
    gm.sib_own()
    gm.sib_ring()
    gm.sib_far()
    for i in range(3):
        raw[i] = dot(rows[...], mix[:, :, i * hcols : (i + 1) * hcols].reshape(ditem, hcols))
    for k in range(1, ntp):
        other = lax.rem(tp + ntp - k, ntp)
        pltpu.make_async_remote_copy(
            src_ref=sums.at[other],
            dst_ref=sums.at[other],
            send_sem=s_send.at[k],
            recv_sem=s_recv.at[k],
            device_id=(seq, lax.rem(tp + k, ntp)),
            device_id_type=MESH,
        ).wait_recv()
    total = sums[0]
    for k in range(1, ntp):
        total = total + sums[k]
    inverse = lax.rsqrt(total[0:1, :] / wide + EPS)
    down = jnp.broadcast_to(inverse, (HD, nslot)).T
    for h in range(heads):
        span = slice(h * HD, (h + 1) * HD)
        kt[seq, span, :] = (raw[1, :, span].T * inverse).astype(BF)
        val[seq, :, span] = (raw[2, :, span] * down).astype(BF)
        query[:, span] = (raw[0, :, span] * (down * (LOG2E / math.sqrt(HD)))).astype(BF)
    gk = PairFirst(over_seq, kt, (0, hcols // 2, kt.shape[1]), k_send, k_recv)
    gv = RingFirst(over_seq, val, (0, nslot // 2, nslot), v_send, v_recv)
    gk.start()
    gv.start()

    qpos[...] = dot(place[...], query[...]).astype(BF)
    vpos[...] = dot(place[...], val[seq]).astype(BF)
    kpos_t[...] = dot(kt[seq, :hcols, :], place_t[...]).astype(BF)
    step = min(256, npos)
    for h in range(heads):
        span = slice(h * HD, (h + 1) * HD)
        for i in range(npos // step):
            here, upto = slice(i * step, (i + 1) * step), (i + 1) * step
            score = dot(qpos[here, span], kpos_t[span, :upto])
            cols = lax.broadcasted_iota(jnp.int32, (step, upto), 1) + first_pos
            allowed = (cols <= col_pos[here]) & (cols >= begin[here])
            score = jnp.where(allowed, score, EMPTY)
            largest = jnp.max(score, axis=1, keepdims=True)
            prob = jnp.exp2(score - largest).astype(BF)
            both = dot(prob, jnp.concatenate([vpos[:upto, span], jnp.ones((upto, HD), BF)], axis=1))
            near[h, here, :] = both[:, :HD] / both[:, HD:]
            near_log[h, here, :] = largest + jnp.log(both[:, HD:]) * LOG2E
    top[...] = jnp.full(top.shape, FLOOR, F32)
    accum[...] = jnp.zeros(accum.shape, F32)

    user_here = user_of(jnp.zeros((16, nslot), jnp.int32) + first_pos)
    which = lax.broadcasted_iota(jnp.int32, (16, nslot), 0)
    chosen_rows = (which % USERS == user_here) & (which < 3 * USERS)
    ones = jnp.ones((nslot, HD), BF)
    band = min(128, nslot)

    def attend(ring):
        bias = []
        for i in range(4):
            tail = kt[ring * 4 + i, hcols:, :].astype(F32)
            line = jnp.sum(jnp.where(chosen_rows, tail, 0.0), axis=0, keepdims=True)
            bias.append(jnp.where(jnp.zeros_like(line, jnp.int32) + ring * 4 + i < seq, line, EMPTY))
        for h in range(heads):
            span = slice(h * HD, (h + 1) * HD)
            for b in range(nslot // band):
                here = slice(b * band, (b + 1) * band)
                asked = query[here, span]
                scores = [dot(asked, kt[ring * 4 + i, span, :]) + bias[i] for i in range(4)]
                largest = jnp.maximum(jnp.maximum(scores[0], scores[1]), jnp.maximum(scores[2], scores[3]))
                before = top[h, here]
                after = jnp.maximum(before, jnp.max(largest, axis=1, keepdims=True))
                both = None
                for i in range(4):
                    prob = jnp.exp2(scores[i] - after[:, :1]).astype(BF)
                    part = dot(prob, jnp.concatenate([val[ring * 4 + i, :, span], ones], axis=1))
                    both = part if both is None else both + part
                shrink = jnp.exp2(before - after)
                accum[h, here] = accum[h, here] * jnp.concatenate([shrink, shrink], axis=1) + both
                top[h, here] = after

    def attend_earlier(step):
        other = (ring + step) % 4

        @pl.when(other < ring)
        def _():
            attend(other)

    ring = seq // 4
    gk.from_pair()
    gv.from_ring()
    gv.from_pair()
    gk.sib_own()
    gv.sib_own()
    attend(ring)
    gk.from_ring()
    gv.from_far()
    gv.pair_ring()
    gk.sib_ring()
    gv.sib_ring()
    attend_earlier(3)
    attend_earlier(1)
    gk.from_far()
    gv.pair_far()
    gk.sib_far()
    gv.sib_far()
    attend_earlier(2)

    lane = lax.broadcasted_iota(jnp.int32, (nslot, HD), 1)
    reaches = begin < first_pos
    for h in range(heads):
        span = slice(h * HD, (h + 1) * HD)
        weight = accum[h, :, HD:]
        some = weight > 0.0
        far = accum[h, :, :HD] / jnp.where(some, weight, 1.0)
        far_log = jnp.where(some, top[h] + jnp.log(jnp.where(some, weight, 1.0)) * LOG2E, FLOOR)
        parts = pieces(far_log)
        packed = jnp.where(lane == 0, parts[0], jnp.where(lane == 1, parts[1], jnp.where(lane == 2, parts[2], 0.0)))
        moved = dot(place[...], jnp.concatenate([far.astype(BF), packed.astype(BF)], axis=1))
        far_log = jnp.sum(moved[:, HD:], axis=1, keepdims=True)
        far_log = jnp.where(reaches, far_log, FLOOR)
        near_here = near_log[h]
        both = jnp.maximum(near_here, far_log)
        near_weight = jnp.exp2(near_here - both)
        far_weight = jnp.exp2(far_log - both)
        mean = (near[h] * near_weight + moved[:, :HD] * far_weight) / (near_weight + far_weight)
        out[:, span] = mean.astype(BF)

    for gather in (ga, gx, ge, gm, gk, gv):
        gather.finish()
    for copy in straight + shared:
        copy.wait_send()


def per_device(
    item_states,
    item_gain,
    adapter,
    send_rows,
    hist_slot,
    hist_lengths,
    user_gain,
    w_query,
    w_key,
    w_value,
):
    ntp, nseq = lax.axis_size("tp"), lax.axis_size("seq")
    cap = send_rows.shape[2]
    arows, wide = adapter.shape
    ditem = item_states.shape[1]
    hcols = w_query.shape[1]
    heads = hcols // HD
    npos = hist_slot.shape[0]
    nchosen = nseq * cap
    nslot = ntp * nchosen
    chunks = ditem // HD
    ecols = wide // ntp
    vmem = pl.BlockSpec(memory_space=pltpu.VMEM)
    smem = pl.BlockSpec(memory_space=pltpu.SMEM)
    hbm = pl.BlockSpec(memory_space=pl.ANY)
    dma = pltpu.SemaphoreType.DMA
    scratch = [
        pltpu.VMEM((ntp, arows, wide), BF),
        pltpu.VMEM((ntp * arows, wide), BF),
        pltpu.VMEM((3, wide, hcols), BF),
        pltpu.VMEM((nslot * chunks, HD), F32),
        pltpu.VMEM((nchosen, chunks, HD), BF),
        pltpu.VMEM((nseq, cap, chunks, HD), BF),
        pltpu.VMEM((ntp, nseq, cap, chunks, HD), BF),
        pltpu.VMEM((nslot, ditem), BF),
        pltpu.VMEM((nseq, ntp * arows, 3 * hcols), BF),
        pltpu.VMEM((nseq, ntp * arows, ecols), BF),
        pltpu.VMEM((3, nslot, hcols), F32),
        pltpu.VMEM((ntp, 8, nslot), F32),
        pltpu.VMEM((nslot, hcols), BF),
        pltpu.VMEM((nseq, hcols + 16, nslot), BF),
        pltpu.VMEM((nseq, nslot, hcols), BF),
        pltpu.VMEM((npos, nslot), BF),
        pltpu.VMEM((nslot, npos), BF),
        pltpu.VMEM((npos, hcols), BF),
        pltpu.VMEM((hcols, npos), BF),
        pltpu.VMEM((npos, hcols), BF),
        pltpu.VMEM((heads, npos, HD), F32),
        pltpu.VMEM((heads, npos, HD), F32),
        pltpu.VMEM((heads, nslot, HD), F32),
        pltpu.VMEM((heads, nslot, 2 * HD), F32),
        dma((3,)),
        dma((9,)),
        dma((9,)),
        dma((nseq,)),
        dma((nseq,)),
        dma((ntp,)),
        dma((ntp,)),
        dma((9,)),
        dma((9,)),
        dma((17,)),
        dma((17,)),
        dma((16,)),
        dma((16,)),
        dma((ntp,)),
        dma((ntp,)),
        dma((17,)),
        dma((17,)),
        dma((16,)),
        dma((16,)),
    ]
    return pl.pallas_call(
        kernel,
        out_shape=jax.ShapeDtypeStruct((npos, hcols), BF),
        in_specs=[smem, vmem, vmem, vmem, smem, vmem, vmem] + [hbm] * 3,
        out_specs=vmem,
        scratch_shapes=scratch,
        compiler_params=pltpu.CompilerParams(
            collective_id=0, has_side_effects=True, vmem_limit_bytes=56 * 1024 * 1024
        ),
    )(
        hist_lengths,
        item_states,
        item_gain.reshape(1, -1),
        adapter,
        send_rows.transpose(1, 2, 0).reshape(cap, nseq),
        hist_slot.reshape(-1, HD),
        user_gain.reshape(1, -1),
        w_query,
        w_key,
        w_value,
    )


def solution(mesh):
    in_specs = (
        P(("seq", "tp"), None),
        P(),
        P(("seq", "tp"), None),
        P(None, ("seq", "tp"), None),
        P("seq"),
        P(),
        P(),
        P(None, "tp"),
        P(None, "tp"),
        P(None, "tp"),
    )
    return jax.shard_map(
        per_device, mesh=mesh, in_specs=in_specs, out_specs=P("seq", "tp"), check_vma=False
    )
```

```python
import math

import jax
import jax.numpy as jnp
from jax import lax
from jax.experimental import pallas as pl
from jax.experimental.pallas import tpu as pltpu
from jax.sharding import PartitionSpec as P

MESH = pl.DeviceIdType.MESH
HD = 128
USERS = 4
EPS = 1e-05
LOG2E = 1.4426950408889634
EMPTY = -1e30
FLOOR = -1e25
BF = jnp.bfloat16
F32 = jnp.float32


def dot(a, b):
    return jnp.dot(a, b, preferred_element_type=F32)


class Group:
    def __init__(self, axis):
        s, t = lax.axis_index("seq"), lax.axis_index("tp")
        if axis == "seq":
            ring, pair, core = s // 4, (s // 2) % 2, s % 2
            self.block = lambda dr=0, dp=0, ds=0: (
                ((ring + dr) % 4) * 4 + ((pair + dp) % 2) * 2 + (core + ds) % 2
            )
            self.device = lambda *d: (self.block(*d), t)
            self.cores = True
        else:
            ring, pair = t // 2, t % 2
            self.block = lambda dr=0, dp=0: ((ring + dr) % 4) * 2 + (pair + dp) % 2
            self.device = lambda *d: (s, self.block(*d))
            self.cores = False
        self.right, self.left, self.pair = self.device(1, 0), self.device(3, 0), self.device(0, 1)
        self.sib = self.device(0, 0, 1) if self.cores else None


class Gather:
    def __init__(self, group, buf, half, send, recv):
        self.g, self.buf, self.half, self.send, self.recv = group, buf, half, send, recv
        self.count, self.sent = 0, []

    def view(self, index, part=None):
        ref = self.buf.at[index]
        if part is None:
            return ref
        axis, cut, end = self.half
        piece = pl.ds(0, cut) if part == 0 else pl.ds(cut, end - cut)
        return ref.at[(slice(None),) * axis + (piece,)]

    def push(self, index, device, slot, part=None, source=None):
        ref = self.view(index, part)
        copy = pltpu.make_async_remote_copy(
            src_ref=ref if source is None else source,
            dst_ref=ref,
            send_sem=self.send.at[self.count],
            recv_sem=self.recv.at[slot],
            device_id=device,
            device_id_type=MESH,
        )
        copy.start()
        self.count += 1
        self.sent.append(copy)

    def got(self, index, slot, part=None):
        ref = self.view(index, part)
        pltpu.make_async_remote_copy(
            src_ref=ref,
            dst_ref=ref,
            send_sem=self.send.at[0],
            recv_sem=self.recv.at[slot],
            device_id=self.g.right,
            device_id_type=MESH,
        ).wait_recv()

    def finish(self):
        for copy in self.sent:
            copy.wait_send()


class PairFirst(Gather):
    def start(self, for_pair=None):
        g = self.g
        own = g.block()
        self.push(own, g.pair, 0, source=for_pair)
        self.push(own, g.right, 1)
        self.push(own, g.left, 3)
        if g.cores:
            self.push(own, g.sib, 9)

    def from_pair(self):
        g = self.g
        block = g.block(0, 1)
        self.got(block, 0)
        self.push(block, g.right, 2)
        self.push(block, g.left, 4)
        if g.cores:
            self.push(block, g.sib, 10)

    def from_ring(self):
        g = self.g
        for dp in (0, 1):
            block = g.block(3, dp)
            self.got(block, 1 + dp)
            self.push(block, g.right, 5 + dp, 0)
            if g.cores:
                self.push(block, g.sib, 11 + dp)
            block = g.block(1, dp)
            self.got(block, 3 + dp)
            self.push(block, g.left, 7 + dp, 1)
            if g.cores:
                self.push(block, g.sib, 13 + dp)

    def from_far(self):
        g = self.g
        for dp in (0, 1):
            block = g.block(2, dp)
            self.got(block, 5 + dp, 0)
            self.got(block, 7 + dp, 1)
            if g.cores:
                self.push(block, g.sib, 15 + dp)

    def sib_own(self):
        for dp in (0, 1):
            self.got(self.g.block(0, dp, 1), 9 + dp)

    def sib_ring(self):
        for dp in (0, 1):
            self.got(self.g.block(3, dp, 1), 11 + dp)
            self.got(self.g.block(1, dp, 1), 13 + dp)

    def sib_far(self):
        for dp in (0, 1):
            self.got(self.g.block(2, dp, 1), 15 + dp)


def pieces(values):
    first = values.astype(BF).astype(F32)
    second = (values - first).astype(BF).astype(F32)
    return first, second, values - first - second


def kernel(
    lengths,
    items,
    item_gain,
    adapter,
    picks,
    slots,
    user_gain,
    w_query,
    w_key,
    w_value,
    out,
    abuf,
    scaled,
    weights,
    spread,
    xs,
    xa,
    xb,
    rows,
    mix,
    ebuf,
    raw,
    sums,
    query,
    kown,
    vown,
    asked,
    kt,
    val,
    means,
    logs,
    place,
    place_t,
    qpos,
    kpos_t,
    vpos,
    near,
    near_log,
    top,
    accum,
    w_sem,
    a_send,
    a_recv,
    r_send,
    r_recv,
    c_send,
    c_recv,
    x_send,
    x_recv,
    m_send,
    m_recv,
    e_send,
    e_recv,
    s_send,
    s_recv,
    k_send,
    k_recv,
    v_send,
    v_recv,
    p_send,
    p_recv,
):
    seq, tp = lax.axis_index("seq"), lax.axis_index("tp")
    nseq, ntp = lax.axis_size("seq"), lax.axis_size("tp")
    wide = adapter.shape[1]
    nslot, ditem = rows.shape
    chunks = ditem // HD
    ecols = ebuf.shape[2]
    hcols = w_query.shape[1]
    heads = hcols // HD
    npos = out.shape[0]
    nchosen = xs.shape[0]
    cap = nchosen // nseq
    first_pos = seq * npos

    loads = []
    for i, ref in enumerate((w_query, w_key, w_value)):
        load = pltpu.make_async_copy(ref, weights.at[i], w_sem.at[i])
        load.start()
        loads.append(load)

    barrier = pltpu.get_barrier_semaphore()
    for k in range(1, ntp):
        peer = (seq, lax.rem(tp + k, ntp))
        pl.semaphore_signal(barrier, inc=1, device_id=peer, device_id_type=MESH)
    for k in range(1, nseq):
        peer = (lax.rem(seq + k, nseq), tp)
        pl.semaphore_signal(barrier, inc=1, device_id=peer, device_id_type=MESH)

    which = lax.broadcasted_iota(jnp.int32, (nchosen, 1), 0)
    column = jnp.zeros((nchosen, 1), jnp.int32)
    for r in range(nchosen):
        column = jnp.where(which == r, picks[r % cap, r // cap], column)
    pick = (lax.broadcasted_iota(jnp.int32, (nchosen, items.shape[0]), 1) == column).astype(BF)
    chosen = dot(pick, items[...])
    factor = lax.rsqrt(jnp.mean(chosen * chosen, axis=1, keepdims=True) + EPS)
    chosen = chosen * factor * item_gain[...]
    for k in range(chunks):
        spread[pl.ds(k, nchosen, stride=chunks), :] = chosen[:, k * HD : (k + 1) * HD]
    xs[...] = spread[...].reshape(nchosen, chunks, HD).astype(BF)

    pl.semaphore_wait(barrier, ntp + nseq - 2)

    over_tp, over_seq = Group("tp"), Group("seq")
    arows = adapter.shape[0]

    abuf[tp] = adapter[...]
    ga = PairFirst(over_tp, abuf, (1, wide // 2, wide), a_send, a_recv)
    ga.start()

    def columns_of(index):
        return adapter.at[:, pl.ds(pl.multiple_of(index * ecols, HD), ecols)]

    def column_copy(k, peer, source):
        return pltpu.make_async_remote_copy(
            src_ref=columns_of(peer),
            dst_ref=ebuf.at[seq, pl.ds(pl.multiple_of(source * arows, arows), arows)],
            send_sem=c_send.at[k],
            recv_sem=c_recv.at[k],
            device_id=(seq, peer),
            device_id_type=MESH,
        )

    def routed_copy(k, peer, source):
        return pltpu.make_async_remote_copy(
            src_ref=xs.at[pl.ds(peer * cap, cap)],
            dst_ref=xa.at[source],
            send_sem=r_send.at[k],
            recv_sem=r_recv.at[k],
            device_id=(peer, tp),
            device_id_type=MESH,
        )

    straight = []
    for k in range(1, ntp):
        straight.append(column_copy(k, lax.rem(tp + k, ntp), tp))
        straight[-1].start()
    for k in range(1, nseq):
        straight.append(routed_copy(k, lax.rem(seq + k, nseq), seq))
        straight[-1].start()
    xa[seq] = xs[pl.ds(seq * cap, cap)]
    ebuf[seq, pl.ds(pl.multiple_of(tp * arows, arows), arows), :] = adapter[
        :, pl.ds(pl.multiple_of(tp * ecols, HD), ecols)
    ]

    origin = slots[...] // cap
    spot = ((origin % ntp) * nseq + origin // ntp) * cap + slots[...] % cap
    groups = spot.shape[0]
    spot_t = jnp.concatenate([spot.astype(F32), jnp.zeros((HD - groups, HD), F32)], axis=0).T.astype(jnp.int32)
    for k in range(groups):
        here = slice(k * HD, (k + 1) * HD)
        place_t[:, here] = (lax.broadcasted_iota(jnp.int32, (nslot, HD), 0) == spot[k : k + 1, :]).astype(BF)
        place[here, :] = (lax.broadcasted_iota(jnp.int32, (HD, nslot), 1) == spot_t[:, k : k + 1]).astype(BF)

    ga.from_pair()
    for k in range(1, ntp):
        column_copy(k, lax.rem(tp + k, ntp), lax.rem(tp + ntp - k, ntp)).wait_recv()
    ge = PairFirst(over_seq, ebuf, (0, ntp * arows // 2, ntp * arows), e_send, e_recv)
    ge.start()
    for k in range(1, nseq):
        routed_copy(k, lax.rem(seq + k, nseq), lax.rem(seq + nseq - k, nseq)).wait_recv()
    xb[tp] = xa[...]
    gx = PairFirst(over_tp, xb, (0, nseq // 2, nseq), x_send, x_recv)
    gx.start()
    ga.from_ring()
    ge.from_pair()

    def lay_out(block):
        size = nchosen * chunks
        spread[...] = xb[block].reshape(size, HD).astype(F32)
        first = pl.multiple_of(block * nchosen, nchosen)
        for k in range(chunks):
            piece = spread[pl.ds(k, nchosen, stride=chunks), :]
            rows[pl.ds(first, nchosen), k * HD : (k + 1) * HD] = piece.astype(BF)

    ends = [lengths[0]]
    for u in range(1, USERS):
        ends.append(ends[-1] + lengths[u])
    row_pos = lax.broadcasted_iota(jnp.int32, (1, npos), 1) + first_pos
    col_pos = lax.broadcasted_iota(jnp.int32, (npos, 1), 0) + first_pos

    def user_of(pos):
        total = jnp.zeros_like(pos)
        for end in ends:
            total = total + jnp.where(pos >= end, 1, 0)
        return total

    begin = jnp.zeros_like(col_pos)
    for end in ends:
        begin = jnp.maximum(begin, jnp.where(col_pos >= end, end, 0))
    belongs = lax.broadcasted_iota(jnp.int32, (16, npos), 0) % USERS == user_of(row_pos)
    held = dot(belongs.astype(BF), place[...])
    weigh = jnp.where(held > 0.5, jnp.log(jnp.maximum(held, 1.0)) * LOG2E, EMPTY)
    parts = pieces(weigh)
    part = lax.broadcasted_iota(jnp.int32, (16, nslot), 0) // USERS
    weigh = jnp.where(part == 0, parts[0], jnp.where(part == 1, parts[1], jnp.where(part == 2, parts[2], 0.0)))
    for h in range(heads):
        kown[h, HD:, :] = weigh.astype(BF)

    ga.from_far()
    arows = ntp * arows
    scaled[...] = (abuf[...].reshape(arows, wide).astype(F32) * user_gain[...]).astype(BF)
    for i, load in enumerate(loads):
        load.wait()
        mix[seq, :, i * hcols : (i + 1) * hcols] = dot(scaled[...], weights[i]).astype(BF)
    gm = PairFirst(over_seq, mix, (0, arows // 2, arows), m_send, m_recv)
    gm.start()

    gx.from_pair()
    ge.from_ring()
    lay_out(over_tp.block())
    lay_out(over_tp.block(0, 1))
    gm.from_pair()
    ge.from_far()
    gx.from_ring()
    for dp in (0, 1):
        lay_out(over_tp.block(3, dp))
        lay_out(over_tp.block(1, dp))
    gm.from_ring()
    gx.from_far()
    for dp in (0, 1):
        lay_out(over_tp.block(2, dp))
    ge.sib_own()
    ge.sib_ring()
    ge.sib_far()

    square = jnp.zeros((nslot, HD), F32)
    tile = min(256, ecols)
    for j in range(ecols // tile):
        emb = dot(rows[...], ebuf[:, :, j * tile : (j + 1) * tile].reshape(ditem, tile))
        for i in range(tile // HD):
            piece = emb[:, i * HD : (i + 1) * HD]
            square = square + piece * piece
    sums[tp] = jnp.broadcast_to(jnp.sum(square.T, axis=0, keepdims=True), (8, nslot))
    shared = []
    for k in range(1, ntp):
        copy = pltpu.make_async_remote_copy(
            src_ref=sums.at[tp],
            dst_ref=sums.at[tp],
            send_sem=s_send.at[k],
            recv_sem=s_recv.at[k],
            device_id=(seq, lax.rem(tp + k, ntp)),
            device_id_type=MESH,
        )
        copy.start()
        shared.append(copy)
    gm.from_far()
    gm.sib_own()
    gm.sib_ring()
    gm.sib_far()
    for i in range(3):
        raw[i] = dot(rows[...], mix[:, :, i * hcols : (i + 1) * hcols].reshape(ditem, hcols))
    for k in range(1, ntp):
        other = lax.rem(tp + ntp - k, ntp)
        pltpu.make_async_remote_copy(
            src_ref=sums.at[other],
            dst_ref=sums.at[other],
            send_sem=s_send.at[k],
            recv_sem=s_recv.at[k],
            device_id=(seq, lax.rem(tp + k, ntp)),
            device_id_type=MESH,
        ).wait_recv()
    total = sums[0]
    for k in range(1, ntp):
        total = total + sums[k]
    inverse = lax.rsqrt(total[0:1, :] / wide + EPS)
    down = jnp.broadcast_to(inverse, (HD, nslot)).T
    mine = (seq // 2) % 2
    theirs = 1 - mine
    for h in range(heads):
        kown[h, :HD, :] = (raw[1, :, h * HD : (h + 1) * HD].T * inverse).astype(BF)
    kt[seq] = kown[mine]
    gk = PairFirst(over_seq, kt, (0, 64, kt.shape[1]), k_send, k_recv)
    gk.start(kown.at[theirs])
    for h in range(heads):
        vown[h] = (raw[2, :, h * HD : (h + 1) * HD] * down).astype(BF)
    val[seq] = vown[mine]
    gv = PairFirst(over_seq, val, (0, nslot // 2, nslot), v_send, v_recv)
    gv.start(vown.at[theirs])
    for h in range(heads):
        query[h] = (raw[0, :, h * HD : (h + 1) * HD] * (down * (LOG2E / math.sqrt(HD)))).astype(BF)

    def to_pair(k, source, target):
        return pltpu.make_async_remote_copy(
            src_ref=source,
            dst_ref=target,
            send_sem=p_send.at[k],
            recv_sem=p_recv.at[k],
            device_id=over_seq.pair,
            device_id_type=MESH,
        )

    asking = to_pair(0, query.at[theirs], asked.at[1])
    asking.start()
    asked[0] = query[mine]

    step = min(256, npos)

    def attend_near(h):
        qpos[...] = dot(place[...], query[h]).astype(BF)
        vpos[...] = dot(place[...], vown[h]).astype(BF)
        kpos_t[...] = dot(kown[h, :HD, :], place_t[...]).astype(BF)
        for i in range(npos // step):
            here, upto = slice(i * step, (i + 1) * step), (i + 1) * step
            score = dot(qpos[here], kpos_t[:, :upto])
            cols = lax.broadcasted_iota(jnp.int32, (step, upto), 1) + first_pos
            allowed = (cols <= col_pos[here]) & (cols >= begin[here])
            score = jnp.where(allowed, score, EMPTY)
            largest = jnp.max(score, axis=1, keepdims=True)
            prob = jnp.exp2(score - largest).astype(BF)
            both = dot(prob, jnp.concatenate([vpos[:upto], jnp.ones((upto, HD), BF)], axis=1))
            near[h, here, :] = both[:, :HD] / both[:, HD:]
            near_log[h, here, :] = largest + jnp.log(both[:, HD:]) * LOG2E

    top[...] = jnp.full(top.shape, FLOOR, F32)
    accum[...] = jnp.zeros(accum.shape, F32)

    which = lax.broadcasted_iota(jnp.int32, (16, nslot), 0)
    ones = jnp.ones((nslot, HD), BF)
    band = min(128, nslot)
    sides = (over_seq.block(), over_seq.block(0, 1))

    def attend(ring, j):
        user_here = user_of(jnp.zeros((16, nslot), jnp.int32) + sides[j] * npos)
        chosen_rows = (which % USERS == user_here) & (which < 3 * USERS)
        bias = []
        for i in range(4):
            tail = kt[ring * 4 + i, HD:, :].astype(F32)
            line = jnp.sum(jnp.where(chosen_rows, tail, 0.0), axis=0, keepdims=True)
            bias.append(jnp.where(jnp.zeros_like(line, jnp.int32) + ring * 4 + i < sides[j], line, EMPTY))
        for b in range(nslot // band):
            here = slice(b * band, (b + 1) * band)
            scores = [dot(asked[j, here], kt[ring * 4 + i, :HD, :]) + bias[i] for i in range(4)]
            largest = jnp.maximum(jnp.maximum(scores[0], scores[1]), jnp.maximum(scores[2], scores[3]))
            before = top[j, here]
            after = jnp.maximum(before, jnp.max(largest, axis=1, keepdims=True))
            both = None
            for i in range(4):
                prob = jnp.exp2(scores[i] - after[:, :1]).astype(BF)
                part = dot(prob, jnp.concatenate([val[ring * 4 + i], ones], axis=1))
                both = part if both is None else both + part
            shrink = jnp.exp2(before - after)
            accum[j, here] = accum[j, here] * jnp.concatenate([shrink, shrink], axis=1) + both
            top[j, here] = after

    def attend_earlier(step, *js):
        other = (ring + step) % 4

        @pl.when(other < ring)
        def _():
            for j in js:
                attend(other, j)

    def far_part(j):
        weight = accum[j, :, HD:]
        some = weight > 0.0
        mean = accum[j, :, :HD] / jnp.where(some, weight, 1.0)
        log = jnp.where(some, top[j] + jnp.log(jnp.where(some, weight, 1.0)) * LOG2E, FLOOR)
        return mean.astype(BF), log

    lane = lax.broadcasted_iota(jnp.int32, (nslot, HD), 1)
    reaches = begin < first_pos

    def finish(h, mean, log):
        parts = pieces(log)
        packed = jnp.where(lane == 0, parts[0], jnp.where(lane == 1, parts[1], jnp.where(lane == 2, parts[2], 0.0)))
        moved = dot(place[...], jnp.concatenate([mean, packed.astype(BF)], axis=1))
        far_log = jnp.sum(moved[:, HD:], axis=1, keepdims=True)
        far_log = jnp.where(reaches, far_log, FLOOR)
        near_here = near_log[h]
        most = jnp.maximum(near_here, far_log)
        near_weight = jnp.exp2(near_here - most)
        far_weight = jnp.exp2(far_log - most)
        result = (near[h] * near_weight + moved[:, :HD] * far_weight) / (near_weight + far_weight)
        out[:, pl.ds(pl.multiple_of(h * HD, HD), HD)] = result.astype(BF)

    ring = seq // 4
    attend_near(0)
    gk.from_pair()
    gv.from_pair()
    attend_near(1)
    asking.wait_recv()
    gk.sib_own()
    gv.sib_own()
    attend(ring, 0)
    attend(ring, 1)
    gk.from_ring()
    gv.from_ring()
    gk.sib_ring()
    gv.sib_ring()
    attend_earlier(3, 0, 1)
    attend_earlier(1, 0, 1)
    gk.from_far()
    gv.from_far()
    gk.sib_far()
    gv.sib_far()
    attend_earlier(2, 1)
    mean, log = far_part(1)
    means[0] = mean
    logs[0] = log.T[:8]
    answers = [to_pair(1, means.at[0], means.at[1]), to_pair(2, logs.at[0], logs.at[1])]
    for copy in answers:
        copy.start()
    attend_earlier(2, 0)
    finish(mine, *far_part(0))
    for copy in answers:
        copy.wait_recv()
    finish(theirs, means[1], jnp.broadcast_to(logs[1, 0:1, :], (HD, nslot)).T)

    for gather in (ga, gx, ge, gm, gk, gv):
        gather.finish()
    for copy in straight + shared + [asking] + answers:
        copy.wait_send()


def per_device(
    item_states,
    item_gain,
    adapter,
    send_rows,
    hist_slot,
    hist_lengths,
    user_gain,
    w_query,
    w_key,
    w_value,
):
    ntp, nseq = lax.axis_size("tp"), lax.axis_size("seq")
    cap = send_rows.shape[2]
    arows, wide = adapter.shape
    ditem = item_states.shape[1]
    hcols = w_query.shape[1]
    heads = hcols // HD
    npos = hist_slot.shape[0]
    nchosen = nseq * cap
    nslot = ntp * nchosen
    chunks = ditem // HD
    ecols = wide // ntp
    vmem = pl.BlockSpec(memory_space=pltpu.VMEM)
    smem = pl.BlockSpec(memory_space=pltpu.SMEM)
    hbm = pl.BlockSpec(memory_space=pl.ANY)
    dma = pltpu.SemaphoreType.DMA
    scratch = [
        pltpu.VMEM((ntp, arows, wide), BF),
        pltpu.VMEM((ntp * arows, wide), BF),
        pltpu.VMEM((3, wide, hcols), BF),
        pltpu.VMEM((nchosen * chunks, HD), F32),
        pltpu.VMEM((nchosen, chunks, HD), BF),
        pltpu.VMEM((nseq, cap, chunks, HD), BF),
        pltpu.VMEM((ntp, nseq, cap, chunks, HD), BF),
        pltpu.VMEM((nslot, ditem), BF),
        pltpu.VMEM((nseq, ntp * arows, 3 * hcols), BF),
        pltpu.VMEM((nseq, ntp * arows, ecols), BF),
        pltpu.VMEM((3, nslot, hcols), F32),
        pltpu.VMEM((ntp, 8, nslot), F32),
        pltpu.VMEM((heads, nslot, HD), BF),
        pltpu.VMEM((heads, HD + 16, nslot), BF),
        pltpu.VMEM((heads, nslot, HD), BF),
        pltpu.VMEM((2, nslot, HD), BF),
        pltpu.VMEM((nseq, HD + 16, nslot), BF),
        pltpu.VMEM((nseq, nslot, HD), BF),
        pltpu.VMEM((2, nslot, HD), BF),
        pltpu.VMEM((2, 8, nslot), F32),
        pltpu.VMEM((npos, nslot), BF),
        pltpu.VMEM((nslot, npos), BF),
        pltpu.VMEM((npos, HD), BF),
        pltpu.VMEM((HD, npos), BF),
        pltpu.VMEM((npos, HD), BF),
        pltpu.VMEM((heads, npos, HD), F32),
        pltpu.VMEM((heads, npos, HD), F32),
        pltpu.VMEM((heads, nslot, HD), F32),
        pltpu.VMEM((heads, nslot, 2 * HD), F32),
        dma((3,)),
        dma((9,)),
        dma((9,)),
        dma((nseq,)),
        dma((nseq,)),
        dma((ntp,)),
        dma((ntp,)),
        dma((9,)),
        dma((9,)),
        dma((17,)),
        dma((17,)),
        dma((17,)),
        dma((17,)),
        dma((ntp,)),
        dma((ntp,)),
        dma((17,)),
        dma((17,)),
        dma((17,)),
        dma((17,)),
        dma((3,)),
        dma((3,)),
    ]
    return pl.pallas_call(
        kernel,
        out_shape=jax.ShapeDtypeStruct((npos, hcols), BF),
        in_specs=[smem, vmem, vmem, vmem, smem, vmem, vmem] + [hbm] * 3,
        out_specs=vmem,
        scratch_shapes=scratch,
        compiler_params=pltpu.CompilerParams(
            collective_id=0, has_side_effects=True, vmem_limit_bytes=56 * 1024 * 1024
        ),
    )(
        hist_lengths,
        item_states,
        item_gain.reshape(1, -1),
        adapter,
        send_rows.transpose(1, 2, 0).reshape(cap, nseq),
        hist_slot.reshape(-1, HD),
        user_gain.reshape(1, -1),
        w_query,
        w_key,
        w_value,
    )


def solution(mesh):
    in_specs = (
        P(("seq", "tp"), None),
        P(),
        P(("seq", "tp"), None),
        P(None, ("seq", "tp"), None),
        P("seq"),
        P(),
        P(),
        P(None, "tp"),
        P(None, "tp"),
        P(None, "tp"),
    )
    return jax.shard_map(
        per_device, mesh=mesh, in_specs=in_specs, out_specs=P("seq", "tp"), check_vma=False
    )
```

```python
import math

import jax
import jax.numpy as jnp
from jax import lax
from jax.experimental import pallas as pl
from jax.experimental.pallas import tpu as pltpu
from jax.sharding import PartitionSpec as P

MESH = pl.DeviceIdType.MESH
HD = 128
USERS = 4
EPS = 1e-05
LOG2E = 1.4426950408889634
EMPTY = -1e30
FLOOR = -1e25
BF = jnp.bfloat16
F32 = jnp.float32


def dot(a, b):
    return jnp.dot(a, b, preferred_element_type=F32)


class Group:
    def __init__(self, axis):
        s, t = lax.axis_index("seq"), lax.axis_index("tp")
        if axis == "seq":
            ring, pair, core = s // 4, (s // 2) % 2, s % 2
            self.block = lambda dr=0, dp=0, ds=0: (
                ((ring + dr) % 4) * 4 + ((pair + dp) % 2) * 2 + (core + ds) % 2
            )
            self.device = lambda *d: (self.block(*d), t)
            self.cores = True
        else:
            ring, pair = t // 2, t % 2
            self.block = lambda dr=0, dp=0: ((ring + dr) % 4) * 2 + (pair + dp) % 2
            self.device = lambda *d: (s, self.block(*d))
            self.cores = False
        self.right, self.left, self.pair = self.device(1, 0), self.device(3, 0), self.device(0, 1)
        self.sib = self.device(0, 0, 1) if self.cores else None


class Gather:
    def __init__(self, group, base, half, send, recv):
        self.g, self.base, self.half, self.send, self.recv = group, base, half, send, recv
        self.count, self.sent = 0, []

    def view(self, index, part=None):
        ref = self.base(index)
        if part is None:
            return ref
        axis, cut, end = self.half
        piece = pl.ds(0, cut) if part == 0 else pl.ds(cut, end - cut)
        return ref.at[(slice(None),) * axis + (piece,)]

    def push(self, index, device, slot, part=None, source=None):
        ref = self.view(index, part)
        copy = pltpu.make_async_remote_copy(
            src_ref=ref if source is None else source,
            dst_ref=ref,
            send_sem=self.send.at[self.count],
            recv_sem=self.recv.at[slot],
            device_id=device,
            device_id_type=MESH,
        )
        copy.start()
        self.count += 1
        self.sent.append(copy)

    def got(self, index, slot, part=None):
        ref = self.view(index, part)
        pltpu.make_async_remote_copy(
            src_ref=ref,
            dst_ref=ref,
            send_sem=self.send.at[0],
            recv_sem=self.recv.at[slot],
            device_id=self.g.right,
            device_id_type=MESH,
        ).wait_recv()

    def finish(self):
        for copy in self.sent:
            copy.wait_send()


class PairFirst(Gather):
    def start(self, for_pair=None):
        g = self.g
        own = g.block()
        self.push(own, g.pair, 0, source=for_pair)
        self.push(own, g.right, 1)
        self.push(own, g.left, 3)
        if g.cores:
            self.push(own, g.sib, 9)

    def from_pair(self):
        g = self.g
        block = g.block(0, 1)
        self.got(block, 0)
        self.push(block, g.right, 2)
        self.push(block, g.left, 4)
        if g.cores:
            self.push(block, g.sib, 10)

    def from_ring(self, dps=(0, 1)):
        g = self.g
        for dp in dps:
            block = g.block(3, dp)
            self.got(block, 1 + dp)
            self.push(block, g.right, 5 + dp, 0)
            if g.cores:
                self.push(block, g.sib, 11 + dp)
            block = g.block(1, dp)
            self.got(block, 3 + dp)
            self.push(block, g.left, 7 + dp, 1)
            if g.cores:
                self.push(block, g.sib, 13 + dp)

    def from_far(self):
        g = self.g
        for dp in (0, 1):
            block = g.block(2, dp)
            self.got(block, 5 + dp, 0)
            self.got(block, 7 + dp, 1)
            if g.cores:
                self.push(block, g.sib, 15 + dp)

    def sib_own(self):
        for dp in (0, 1):
            self.got(self.g.block(0, dp, 1), 9 + dp)

    def sib_ring(self):
        for dp in (0, 1):
            self.got(self.g.block(3, dp, 1), 11 + dp)
            self.got(self.g.block(1, dp, 1), 13 + dp)

    def sib_far(self):
        for dp in (0, 1):
            self.got(self.g.block(2, dp, 1), 15 + dp)


class RingFirst(Gather):
    def start(self):
        g = self.g
        own = g.block()
        self.push(own, g.right, 1)
        self.push(own, g.left, 2)
        self.push(own, g.pair, 0)
        if g.cores:
            self.push(own, g.sib, 8)

    def from_pair(self):
        g = self.g
        block = g.block(0, 1)
        self.got(block, 0)
        if g.cores:
            self.push(block, g.sib, 9)

    def from_ring(self):
        g = self.g
        block = g.block(3, 0)
        self.got(block, 1)
        self.push(block, g.right, 3, 0)
        self.push(block, g.pair, 5)
        if g.cores:
            self.push(block, g.sib, 10)
        block = g.block(1, 0)
        self.got(block, 2)
        self.push(block, g.left, 4, 1)
        self.push(block, g.pair, 6)
        if g.cores:
            self.push(block, g.sib, 11)

    def from_far(self):
        g = self.g
        block = g.block(2, 0)
        self.got(block, 3, 0)
        self.got(block, 4, 1)
        self.push(block, g.pair, 7)
        if g.cores:
            self.push(block, g.sib, 12)

    def pair_ring(self):
        g = self.g
        for dr, slot in ((3, 5), (1, 6)):
            block = g.block(dr, 1)
            self.got(block, slot)
            if g.cores:
                self.push(block, g.sib, 8 + slot)

    def pair_far(self):
        g = self.g
        block = g.block(2, 1)
        self.got(block, 7)
        if g.cores:
            self.push(block, g.sib, 15)

    def sib_own(self):
        g = self.g
        self.got(g.block(0, 0, 1), 8)
        self.got(g.block(0, 1, 1), 9)

    def sib_ring(self):
        g = self.g
        self.got(g.block(3, 0, 1), 10)
        self.got(g.block(1, 0, 1), 11)
        self.got(g.block(3, 1, 1), 13)
        self.got(g.block(1, 1, 1), 14)

    def sib_far(self):
        g = self.g
        self.got(g.block(2, 0, 1), 12)
        self.got(g.block(2, 1, 1), 15)


def pieces(values):
    first = values.astype(BF).astype(F32)
    second = (values - first).astype(BF).astype(F32)
    return first, second, values - first - second


def kernel(
    lengths,
    items,
    item_gain,
    adapter,
    picks,
    slots,
    user_gain,
    w_query,
    w_key,
    w_value,
    out,
    abuf,
    scaled,
    weights,
    spread,
    xs,
    xb,
    rows,
    mix,
    ebuf,
    raw,
    sums,
    query,
    kown,
    vown,
    asked,
    kt,
    val,
    means,
    logs,
    place,
    place_t,
    qpos,
    kpos_t,
    vpos,
    near,
    near_log,
    top,
    accum,
    w_sem,
    a_send,
    a_recv,
    b_send,
    b_recv,
    r_send,
    r_recv,
    c_send,
    c_recv,
    x_send,
    x_recv,
    m_send,
    m_recv,
    n_send,
    n_recv,
    o_send,
    o_recv,
    e_send,
    e_recv,
    s_send,
    s_recv,
    k_send,
    k_recv,
    v_send,
    v_recv,
    p_send,
    p_recv,
):
    seq, tp = lax.axis_index("seq"), lax.axis_index("tp")
    nseq, ntp = lax.axis_size("seq"), lax.axis_size("tp")
    wide = adapter.shape[1]
    nslot, ditem = rows.shape
    chunks = ditem // HD
    ecols = ebuf.shape[2]
    hcols = w_query.shape[1]
    heads = hcols // HD
    npos = out.shape[0]
    nchosen = xs.shape[0]
    cap = nchosen // nseq
    first_pos = seq * npos

    loads = []
    for i, ref in enumerate((w_query, w_key, w_value)):
        load = pltpu.make_async_copy(ref, weights.at[i], w_sem.at[i])
        load.start()
        loads.append(load)

    barrier = pltpu.get_barrier_semaphore()
    for k in range(1, ntp):
        peer = (seq, lax.rem(tp + k, ntp))
        pl.semaphore_signal(barrier, inc=1, device_id=peer, device_id_type=MESH)
    for k in range(1, nseq):
        peer = (lax.rem(seq + k, nseq), tp)
        pl.semaphore_signal(barrier, inc=1, device_id=peer, device_id_type=MESH)

    which = lax.broadcasted_iota(jnp.int32, (nchosen, 1), 0)
    column = jnp.zeros((nchosen, 1), jnp.int32)
    for r in range(nchosen):
        column = jnp.where(which == r, picks[r % cap, r // cap], column)
    pick = (lax.broadcasted_iota(jnp.int32, (nchosen, items.shape[0]), 1) == column).astype(BF)
    chosen = dot(pick, items[...])
    factor = lax.rsqrt(jnp.mean(chosen * chosen, axis=1, keepdims=True) + EPS)
    chosen = chosen * factor * item_gain[...]
    for k in range(chunks):
        spread[pl.ds(k, nchosen, stride=chunks), :] = chosen[:, k * HD : (k + 1) * HD]
    xs[...] = spread[...].reshape(nchosen, chunks, HD).astype(BF)

    pl.semaphore_wait(barrier, ntp + nseq - 2)

    over_tp, over_seq = Group("tp"), Group("seq")
    arows = adapter.shape[0]

    abuf[tp] = adapter[...]
    cut = wide * 3 // 4
    ga = PairFirst(over_tp, lambda i: abuf.at[i, :, :cut], (1, cut // 2, cut), a_send, a_recv)
    ha = RingFirst(
        over_tp, lambda i: abuf.at[i, :, cut:], (1, (wide - cut) // 2, wide - cut), b_send, b_recv
    )
    ga.start()
    ha.start()

    def columns_of(index):
        return adapter.at[:, pl.ds(pl.multiple_of(index * ecols, HD), ecols)]

    def column_copy(k, peer, source):
        return pltpu.make_async_remote_copy(
            src_ref=columns_of(peer),
            dst_ref=ebuf.at[seq, pl.ds(pl.multiple_of(source * arows, arows), arows)],
            send_sem=c_send.at[k],
            recv_sem=c_recv.at[k],
            device_id=(seq, peer),
            device_id_type=MESH,
        )

    def routed_copy(k, source):
        return pltpu.make_async_remote_copy(
            src_ref=xs.at[pl.ds(lax.rem(seq + k, nseq) * cap, cap)],
            dst_ref=xb.at[tp, source],
            send_sem=r_send.at[k],
            recv_sem=r_recv.at[k],
            device_id=(lax.rem(seq + k, nseq), tp),
            device_id_type=MESH,
        )

    straight = []
    for k in range(1, ntp):
        straight.append(column_copy(k, lax.rem(tp + k, ntp), tp))
        straight[-1].start()
    for k in range(1, nseq):
        straight.append(routed_copy(k, seq))
        straight[-1].start()
    xb[tp, seq] = xs[pl.ds(seq * cap, cap)]
    ebuf[seq, pl.ds(pl.multiple_of(tp * arows, arows), arows), :] = adapter[
        :, pl.ds(pl.multiple_of(tp * ecols, HD), ecols)
    ]

    origin = slots[...] // cap
    spot = ((origin % ntp) * nseq + origin // ntp) * cap + slots[...] % cap
    groups = spot.shape[0]
    spot_t = jnp.concatenate([spot.astype(F32), jnp.zeros((HD - groups, HD), F32)], axis=0).T.astype(jnp.int32)
    for k in range(groups):
        here = slice(k * HD, (k + 1) * HD)
        place_t[:, here] = (lax.broadcasted_iota(jnp.int32, (nslot, HD), 0) == spot[k : k + 1, :]).astype(BF)
        place[here, :] = (lax.broadcasted_iota(jnp.int32, (HD, nslot), 1) == spot_t[:, k : k + 1]).astype(BF)

    ga.from_pair()
    ha.from_ring()
    for k in range(1, ntp):
        column_copy(k, lax.rem(tp + k, ntp), lax.rem(tp + ntp - k, ntp)).wait_recv()
    ge = PairFirst(over_seq, lambda i: ebuf.at[i], (0, ntp * arows // 2, ntp * arows), e_send, e_recv)
    ge.start()
    for k in range(1, nseq):
        routed_copy(k, lax.rem(seq + nseq - k, nseq)).wait_recv()
    gx = PairFirst(over_tp, lambda i: xb.at[i], (0, nseq // 2, nseq), x_send, x_recv)
    gx.start()
    ga.from_ring()
    ha.from_far()
    ha.from_pair()

    def lay_out(*block):
        index = over_tp.block(*block)
        size = nchosen * chunks
        spread[...] = xb[index].reshape(size, HD).astype(F32)
        first = pl.multiple_of(index * nchosen, nchosen)
        for k in range(chunks):
            piece = spread[pl.ds(k, nchosen, stride=chunks), :]
            rows[pl.ds(first, nchosen), k * HD : (k + 1) * HD] = piece.astype(BF)

    ends = [lengths[0]]
    for u in range(1, USERS):
        ends.append(ends[-1] + lengths[u])
    row_pos = lax.broadcasted_iota(jnp.int32, (1, npos), 1) + first_pos
    col_pos = lax.broadcasted_iota(jnp.int32, (npos, 1), 0) + first_pos

    def user_of(pos):
        total = jnp.zeros_like(pos)
        for end in ends:
            total = total + jnp.where(pos >= end, 1, 0)
        return total

    begin = jnp.zeros_like(col_pos)
    for end in ends:
        begin = jnp.maximum(begin, jnp.where(col_pos >= end, end, 0))
    belongs = lax.broadcasted_iota(jnp.int32, (16, npos), 0) % USERS == user_of(row_pos)
    held = dot(belongs.astype(BF), place[...])
    weigh = jnp.where(held > 0.5, jnp.log(jnp.maximum(held, 1.0)) * LOG2E, EMPTY)
    parts = pieces(weigh)
    part = lax.broadcasted_iota(jnp.int32, (16, nslot), 0) // USERS
    weigh = jnp.where(part == 0, parts[0], jnp.where(part == 1, parts[1], jnp.where(part == 2, parts[2], 0.0)))
    for h in range(heads):
        kown[h, HD:, :] = weigh.astype(BF)

    ge.from_pair()
    ha.pair_ring()
    ga.from_far()
    ha.pair_far()
    arows = ntp * arows
    scaled[...] = (abuf[...].reshape(arows, wide).astype(F32) * user_gain[...]).astype(BF)

    def part_of(i):
        return lambda index: mix.at[index, :, pl.ds(i * hcols, hcols)]

    def multiply(i):
        loads[i].wait()
        mix[seq, :, i * hcols : (i + 1) * hcols] = dot(scaled[...], weights[i]).astype(BF)

    halves = (0, arows // 2, arows)
    gq = PairFirst(over_seq, part_of(0), halves, m_send, m_recv)
    gm = PairFirst(over_seq, part_of(1), halves, n_send, n_recv)
    gw = RingFirst(over_seq, part_of(2), halves, o_send, o_recv)
    multiply(1)
    gm.start()
    gx.from_pair()
    multiply(2)
    gw.start()
    multiply(0)
    gq.start()
    lay_out()
    lay_out(0, 1)
    gm.from_pair()
    ge.from_ring()
    gx.from_ring()
    gq.from_pair()
    gw.from_ring()
    gw.from_pair()
    for dp in (0, 1):
        lay_out(3, dp)
        lay_out(1, dp)
    ge.from_far()
    gm.from_ring()
    gq.from_ring()
    gw.from_far()
    gw.pair_ring()
    gm.from_far()
    gx.from_far()
    for dp in (0, 1):
        lay_out(2, dp)

    def project(i):
        raw[i] = dot(rows[...], mix[:, :, i * hcols : (i + 1) * hcols].reshape(ditem, hcols))

    mine = (seq // 2) % 2
    theirs = 1 - mine
    gm.sib_own()
    gm.sib_ring()
    gm.sib_far()
    project(1)
    for h in range(heads):
        kown[h, :HD, :] = raw[1, :, h * HD : (h + 1) * HD].T.astype(BF)
    kt[seq] = kown[mine]
    gk = PairFirst(over_seq, lambda i: kt.at[i], (0, 64, kt.shape[1]), k_send, k_recv)
    gk.start(kown.at[theirs])
    ge.sib_own()
    ge.sib_ring()
    ge.sib_far()

    square = jnp.zeros((nslot, HD), F32)
    tile = min(256, ecols)
    for j in range(ecols // tile):
        emb = dot(rows[...], ebuf[:, :, j * tile : (j + 1) * tile].reshape(ditem, tile))
        for i in range(tile // HD):
            piece = emb[:, i * HD : (i + 1) * HD]
            square = square + piece * piece
    sums[tp] = jnp.broadcast_to(jnp.sum(square.T, axis=0, keepdims=True), (8, nslot))
    shared = []
    for k in range(1, ntp):
        copy = pltpu.make_async_remote_copy(
            src_ref=sums.at[tp],
            dst_ref=sums.at[tp],
            send_sem=s_send.at[k],
            recv_sem=s_recv.at[k],
            device_id=(seq, lax.rem(tp + k, ntp)),
            device_id_type=MESH,
        )
        copy.start()
        shared.append(copy)
    gk.from_pair()
    gk.from_ring((0,))
    gq.from_far()
    gw.pair_far()
    for gather in (gw, gq):
        gather.sib_own()
        gather.sib_ring()
        gather.sib_far()
    project(2)
    for k in range(1, ntp):
        other = lax.rem(tp + ntp - k, ntp)
        pltpu.make_async_remote_copy(
            src_ref=sums.at[other],
            dst_ref=sums.at[other],
            send_sem=s_send.at[k],
            recv_sem=s_recv.at[k],
            device_id=(seq, lax.rem(tp + k, ntp)),
            device_id_type=MESH,
        ).wait_recv()
    total = sums[0]
    for k in range(1, ntp):
        total = total + sums[k]
    inverse = lax.rsqrt(total[0:1, :] / wide + EPS)
    down = jnp.broadcast_to(inverse, (HD, nslot)).T
    for h in range(heads):
        vown[h, :nslot] = (raw[2, :, h * HD : (h + 1) * HD] * down).astype(BF)
    line = lax.broadcasted_iota(jnp.int32, (16, HD), 0)
    tiles = nslot // HD
    norms = jnp.zeros((16, HD), F32)
    for r, term in enumerate(pieces(inverse)):
        for k in range(tiles):
            norms = jnp.where(line == r * tiles + k, term[:, k * HD : (k + 1) * HD], norms)
    for h in range(heads):
        vown[h, nslot:] = norms.astype(BF)
    val[seq] = vown[mine]
    gv = PairFirst(over_seq, lambda i: val.at[i], (0, nslot // 2, val.shape[1]), v_send, v_recv)
    gv.start(vown.at[theirs])
    project(0)
    for h in range(heads):
        query[h] = (raw[0, :, h * HD : (h + 1) * HD] * (down * (LOG2E / math.sqrt(HD)))).astype(BF)

    def to_pair(k, source, target):
        return pltpu.make_async_remote_copy(
            src_ref=source,
            dst_ref=target,
            send_sem=p_send.at[k],
            recv_sem=p_recv.at[k],
            device_id=over_seq.pair,
            device_id_type=MESH,
        )

    asking = to_pair(0, query.at[theirs], asked.at[1])
    asking.start()
    asked[0] = query[mine]

    step = min(256, npos)

    def attend_near(h):
        qpos[...] = dot(place[...], query[h]).astype(BF)
        vpos[...] = dot(place[...], vown[h, :nslot]).astype(BF)
        scaled_keys = (kown[h, :HD, :].astype(F32) * inverse).astype(BF)
        kpos_t[...] = dot(scaled_keys, place_t[...]).astype(BF)
        for i in range(npos // step):
            here, upto = slice(i * step, (i + 1) * step), (i + 1) * step
            score = dot(qpos[here], kpos_t[:, :upto])
            cols = lax.broadcasted_iota(jnp.int32, (step, upto), 1) + first_pos
            allowed = (cols <= col_pos[here]) & (cols >= begin[here])
            score = jnp.where(allowed, score, EMPTY)
            largest = jnp.max(score, axis=1, keepdims=True)
            prob = jnp.exp2(score - largest).astype(BF)
            both = dot(prob, jnp.concatenate([vpos[:upto], jnp.ones((upto, HD), BF)], axis=1))
            near[h, here, :] = both[:, :HD] / both[:, HD:]
            near_log[h, here, :] = largest + jnp.log(both[:, HD:]) * LOG2E

    top[...] = jnp.full(top.shape, FLOOR, F32)
    accum[...] = jnp.zeros(accum.shape, F32)

    which = lax.broadcasted_iota(jnp.int32, (16, nslot), 0)
    ones = jnp.ones((nslot, HD), BF)
    band = min(128, nslot)
    sides = (over_seq.block(), over_seq.block(0, 1))

    def attend(ring, j):
        user_here = user_of(jnp.zeros((16, nslot), jnp.int32) + sides[j] * npos)
        chosen_rows = (which % USERS == user_here) & (which < 3 * USERS)
        bias, factor = [], []
        for i in range(4):
            tail = kt[ring * 4 + i, HD:, :].astype(F32)
            held = jnp.sum(jnp.where(chosen_rows, tail, 0.0), axis=0, keepdims=True)
            bias.append(jnp.where(jnp.zeros_like(held, jnp.int32) + ring * 4 + i < sides[j], held, EMPTY))
            tail = val[ring * 4 + i, nslot:, :].astype(F32)
            factor.append(
                jnp.concatenate(
                    [
                        jnp.sum(jnp.where((line % tiles == k) & (line < 3 * tiles), tail, 0.0), axis=0, keepdims=True)
                        for k in range(tiles)
                    ],
                    axis=1,
                )
            )
        for b in range(nslot // band):
            here = slice(b * band, (b + 1) * band)
            scores = [dot(asked[j, here], kt[ring * 4 + i, :HD, :]) * factor[i] + bias[i] for i in range(4)]
            largest = jnp.maximum(jnp.maximum(scores[0], scores[1]), jnp.maximum(scores[2], scores[3]))
            before = top[j, here]
            after = jnp.maximum(before, jnp.max(largest, axis=1, keepdims=True))
            both = None
            for i in range(4):
                prob = jnp.exp2(scores[i] - after[:, :1]).astype(BF)
                part = dot(prob, jnp.concatenate([val[ring * 4 + i, :nslot], ones], axis=1))
                both = part if both is None else both + part
            shrink = jnp.exp2(before - after)
            accum[j, here] = accum[j, here] * jnp.concatenate([shrink, shrink], axis=1) + both
            top[j, here] = after

    def attend_earlier(step, *js):
        other = (ring + step) % 4

        @pl.when(other < ring)
        def _():
            for j in js:
                attend(other, j)

    def far_part(j):
        weight = accum[j, :, HD:]
        some = weight > 0.0
        mean = accum[j, :, :HD] / jnp.where(some, weight, 1.0)
        log = jnp.where(some, top[j] + jnp.log(jnp.where(some, weight, 1.0)) * LOG2E, FLOOR)
        return mean.astype(BF), log

    lane = lax.broadcasted_iota(jnp.int32, (nslot, HD), 1)
    reaches = begin < first_pos

    def finish(h, mean, log):
        parts = pieces(log)
        packed = jnp.where(lane == 0, parts[0], jnp.where(lane == 1, parts[1], jnp.where(lane == 2, parts[2], 0.0)))
        moved = dot(place[...], jnp.concatenate([mean, packed.astype(BF)], axis=1))
        far_log = jnp.sum(moved[:, HD:], axis=1, keepdims=True)
        far_log = jnp.where(reaches, far_log, FLOOR)
        near_here = near_log[h]
        most = jnp.maximum(near_here, far_log)
        near_weight = jnp.exp2(near_here - most)
        far_weight = jnp.exp2(far_log - most)
        result = (near[h] * near_weight + moved[:, :HD] * far_weight) / (near_weight + far_weight)
        out[:, pl.ds(pl.multiple_of(h * HD, HD), HD)] = result.astype(BF)

    ring = seq // 4
    attend_near(0)
    gk.from_ring((1,))
    attend_near(1)
    gv.from_pair()
    gv.from_ring((0,))
    asking.wait_recv()
    gk.sib_own()
    gv.sib_own()
    attend(ring, 1)
    attend(ring, 0)
    gv.from_ring((1,))
    gk.sib_ring()
    gv.sib_ring()
    attend_earlier(3, 1)
    attend_earlier(1, 1)
    gk.from_far()
    gv.from_far()
    attend_earlier(3, 0)
    gk.sib_far()
    gv.sib_far()
    attend_earlier(2, 1)
    mean, log = far_part(1)
    means[0] = mean
    logs[0] = log.T[:8]
    answers = [to_pair(1, means.at[0], means.at[1]), to_pair(2, logs.at[0], logs.at[1])]
    for copy in answers:
        copy.start()
    attend_earlier(1, 0)
    attend_earlier(2, 0)
    finish(mine, *far_part(0))
    for copy in answers:
        copy.wait_recv()
    finish(theirs, means[1], jnp.broadcast_to(logs[1, 0:1, :], (HD, nslot)).T)

    for gather in (ga, ha, gx, ge, gq, gm, gw, gk, gv):
        gather.finish()
    for copy in straight + shared + [asking] + answers:
        copy.wait_send()


def per_device(
    item_states,
    item_gain,
    adapter,
    send_rows,
    hist_slot,
    hist_lengths,
    user_gain,
    w_query,
    w_key,
    w_value,
):
    ntp, nseq = lax.axis_size("tp"), lax.axis_size("seq")
    cap = send_rows.shape[2]
    arows, wide = adapter.shape
    ditem = item_states.shape[1]
    hcols = w_query.shape[1]
    heads = hcols // HD
    npos = hist_slot.shape[0]
    nchosen = nseq * cap
    nslot = ntp * nchosen
    chunks = ditem // HD
    ecols = wide // ntp
    vmem = pl.BlockSpec(memory_space=pltpu.VMEM)
    smem = pl.BlockSpec(memory_space=pltpu.SMEM)
    hbm = pl.BlockSpec(memory_space=pl.ANY)
    dma = pltpu.SemaphoreType.DMA
    scratch = [
        pltpu.VMEM((ntp, arows, wide), BF),
        pltpu.VMEM((ntp * arows, wide), BF),
        pltpu.VMEM((3, wide, hcols), BF),
        pltpu.VMEM((nchosen * chunks, HD), F32),
        pltpu.VMEM((nchosen, chunks, HD), BF),
        pltpu.VMEM((ntp, nseq, cap, chunks, HD), BF),
        pltpu.VMEM((nslot, ditem), BF),
        pltpu.VMEM((nseq, ntp * arows, 3 * hcols), BF),
        pltpu.VMEM((nseq, ntp * arows, ecols), BF),
        pltpu.VMEM((3, nslot, hcols), F32),
        pltpu.VMEM((ntp, 8, nslot), F32),
        pltpu.VMEM((heads, nslot, HD), BF),
        pltpu.VMEM((heads, HD + 16, nslot), BF),
        pltpu.VMEM((heads, nslot + 16, HD), BF),
        pltpu.VMEM((2, nslot, HD), BF),
        pltpu.VMEM((nseq, HD + 16, nslot), BF),
        pltpu.VMEM((nseq, nslot + 16, HD), BF),
        pltpu.VMEM((2, nslot, HD), BF),
        pltpu.VMEM((2, 8, nslot), F32),
        pltpu.VMEM((npos, nslot), BF),
        pltpu.VMEM((nslot, npos), BF),
        pltpu.VMEM((npos, HD), BF),
        pltpu.VMEM((HD, npos), BF),
        pltpu.VMEM((npos, HD), BF),
        pltpu.VMEM((heads, npos, HD), F32),
        pltpu.VMEM((heads, npos, HD), F32),
        pltpu.VMEM((heads, nslot, HD), F32),
        pltpu.VMEM((heads, nslot, 2 * HD), F32),
        dma((3,)),
        dma((9,)),
        dma((9,)),
        dma((8,)),
        dma((8,)),
        dma((nseq,)),
        dma((nseq,)),
        dma((ntp,)),
        dma((ntp,)),
        dma((9,)),
        dma((9,)),
        dma((17,)),
        dma((17,)),
        dma((17,)),
        dma((17,)),
        dma((16,)),
        dma((16,)),
        dma((17,)),
        dma((17,)),
        dma((ntp,)),
        dma((ntp,)),
        dma((17,)),
        dma((17,)),
        dma((17,)),
        dma((17,)),
        dma((3,)),
        dma((3,)),
    ]
    return pl.pallas_call(
        kernel,
        out_shape=jax.ShapeDtypeStruct((npos, hcols), BF),
        in_specs=[smem, vmem, vmem, vmem, smem, vmem, vmem] + [hbm] * 3,
        out_specs=vmem,
        scratch_shapes=scratch,
        compiler_params=pltpu.CompilerParams(
            collective_id=0, has_side_effects=True, vmem_limit_bytes=56 * 1024 * 1024
        ),
    )(
        hist_lengths,
        item_states,
        item_gain.reshape(1, -1),
        adapter,
        send_rows.transpose(1, 2, 0).reshape(cap, nseq),
        hist_slot.reshape(-1, HD),
        user_gain.reshape(1, -1),
        w_query,
        w_key,
        w_value,
    )


def solution(mesh):
    in_specs = (
        P(("seq", "tp"), None),
        P(),
        P(("seq", "tp"), None),
        P(None, ("seq", "tp"), None),
        P("seq"),
        P(),
        P(),
        P(None, "tp"),
        P(None, "tp"),
        P(None, "tp"),
    )
    return jax.shard_map(
        per_device, mesh=mesh, in_specs=in_specs, out_specs=P("seq", "tp"), check_vma=False
    )
```
